32 devices in a mesh: gx: 16 (over z, x, core), gy: 2 (over y).
Axes of the slice: x: 2, y: 2, z: 4, core: 2. Of those that a mesh axis runs over, the one named last changes fastest.
Arguments:
- populations: float32 [19, 64, 64, 128], P(None, 'gx', 'gy'), may hold values from 0 to 1, as said below
- labels: int32 [64, 64, 128], P('gx', 'gy'), may hold values from 0 to 3
- solid_mask: int32 [64, 64, 128], P('gx', 'gy'), may hold values 0 or 1
Outputs:
- new_populations: float32 [19, 64, 64, 128], P(None, 'gx', 'gy')
- phase: float32 [64, 64, 128], P('gx', 'gy')
The draws below stay inside these ranges and needn't reach their ends.
Inputs may be any that keep to these rules, and one draw needn't show every extreme that they name: `populations`: every entry is positive.
All inputs are finite; a program needn't handle non-finite values. No bound on the sum of `solid_mask` on one device may be relied on, other than what follows from the above.
Results may differ from the reference program's by a relative error of at most 0.00011.
Values sent between devices are 32-bit elements; how exact they have to be, the bound alone decides.
A program may use at most 64 MiB of HBM per device.

```python
import jax
import jax.numpy as jnp
import numpy as np
from jax import lax

NZ = 128
STEPS = 2
NX = 64
NY = 64


WEIGHTS_TABLE = [1.0 / 3.0] + [1.0 / 18.0] * 6 + [1.0 / 36.0] * 12


def draw_populations(key, part):
    lattice_weights = jnp.asarray(WEIGHTS_TABLE, jnp.float32).reshape(19, 1, 1, 1)
    noise = jax.random.uniform(key, (19, NX, NY, NZ), jnp.float32, -1.0, 1.0)
    result = lattice_weights * (1.0 + 0.5 * noise)
    return result


def place_ends(drawn, own_key, smallest, top_value):
    extent = drawn.shape
    spot = [jax.random.randint(jax.random.fold_in(own_key, axis), (), 0, extent[axis]) for axis in range(len(extent))]
    drawn = drawn.at[tuple(spot)].set(smallest)
    longest = extent.index(max(extent))
    spot[longest] = (spot[longest] + 1) % extent[longest]
    return drawn.at[tuple(spot)].set(top_value)


def setup_inputs(seed: int = 0) -> dict:
    seeds = jax.random.split(jax.random.key(seed), 4)
    return {
        "populations": draw_populations(jax.random.fold_in(seeds[3], 71), 0),
        "labels": place_ends(jax.random.randint(seeds[1], (NX, NY, NZ), 0, 4), jax.random.fold_in(seeds[1], 1), 0, 3).astype(jnp.int32),
        "solid_mask": place_ends((jax.random.randint(seeds[2], (NX, NY, NZ), 0, 8) < 1).astype(jnp.int32), jax.random.fold_in(seeds[2], 1), 0, 1),
    }


VELOCITY_SET = [(0, 0, 0), (1, 0, 0), (-1, 0, 0), (0, 1, 0), (0, -1, 0), (0, 0, 1), (0, 0, -1), (1, 1, 0), (-1, -1, 0), (1, -1, 0), (-1, 1, 0), (1, 0, 1), (-1, 0, -1), (1, 0, -1), (-1, 0, 1), (0, 1, 1), (0, -1, -1), (0, 1, -1), (0, -1, 1)]
OPPOSITE = [0, 2, 1, 4, 3, 6, 5, 8, 7, 10, 9, 12, 11, 14, 13, 16, 15, 18, 17]
WEIGHTS = [1.0 / 3.0] + [1.0 / 18.0] * 6 + [1.0 / 36.0] * 12
BALANCE = [-1.0 / 3.0] + [1.0 / 18.0] * 6 + [1.0 / 36.0] * 12
RELAX_RATES = [0.0, 0.0, 0.0, 0.0, 1.0, 1.25, 1.25, 1.25, 1.25, 1.25, 1.2, 1.2, 1.2, 1.2, 1.2, 1.2, 1.4, 1.4, 1.4]
SURFACE_COEF = 0.2
SEGREGATION_RATE = 0.7
GRAD_FLOOR = 0.1

def moment_values(ex, ey, ez):
    return [1.0, ex, ey, ez, ex * ex + ey * ey + ez * ez, ex * ex - ey * ey, ey * ey - ez * ez, ex * ey, ex * ez, ey * ez, ex * ex * ey, ex * ex * ez, ey * ey * ex, ey * ey * ez, ez * ez * ex, ez * ez * ey, ex * ex * ey * ey, ex * ex * ez * ez, ey * ey * ez * ez]

def build_collision():
    count = 19
    columns = [moment_values(float(v[0]), float(v[1]), float(v[2])) for v in VELOCITY_SET]
    moments = [[columns[col_index][row_index] for col_index in range(count)] for row_index in range(count)]
    augmented = [moments[row_index][:] + [1.0 if row_index == col_index else 0.0 for col_index in range(count)] for row_index in range(count)]
    for column in range(count):
        pivot_row = column
        for row_index in range(column + 1, count):
            if abs(augmented[row_index][column]) > abs(augmented[pivot_row][column]):
                pivot_row = row_index
        augmented[column], augmented[pivot_row] = (augmented[pivot_row], augmented[column])
        leading = augmented[column][column]
        augmented[column] = [entry / leading for entry in augmented[column]]
        for row_index in range(count):
            if row_index != column:
                factor = augmented[row_index][column]
                if factor != 0.0:
                    augmented[row_index] = [entry - factor * pivot_entry for entry, pivot_entry in zip(augmented[row_index], augmented[column])]
    inverse = [augmented[row_index][count:] for row_index in range(count)]
    result = [[sum((inverse[row_index][inner] * RELAX_RATES[inner] * moments[inner][col_index] for inner in range(count))) for col_index in range(count)] for row_index in range(count)]
    return np.array(result, dtype=np.float32)

def velocity_table():
    return np.array(VELOCITY_SET, dtype=np.float32).T.copy()

def gradient_of(padded, size_x, size_y):
    shape = (size_x, size_y, padded.shape[2])
    grad_x = jnp.zeros(shape, jnp.float32)
    grad_y = jnp.zeros(shape, jnp.float32)
    grad_z = jnp.zeros(shape, jnp.float32)
    for direction in range(1, 19):
        ex, ey, ez = VELOCITY_SET[direction]
        part = padded[1 + ex:1 + ex + size_x, 1 + ey:1 + ey + size_y]
        value = jnp.roll(part, -ez, axis=2)
        factor = 3.0 * WEIGHTS[direction]
        if ex != 0:
            grad_x = grad_x + factor * ex * value
        if ey != 0:
            grad_y = grad_y + factor * ey * value
        if ez != 0:
            grad_z = grad_z + factor * ez * value
    return jnp.stack([grad_x, grad_y, grad_z])

def collide(pops, phase, grad, wall_nodes):
    tail = (1,) * (pops.ndim - 1)
    lattice_weights = jnp.asarray(WEIGHTS, jnp.float32).reshape((19,) + tail)
    balance = jnp.asarray(BALANCE, jnp.float32).reshape((19,) + tail)
    table = jnp.asarray(velocity_table(), jnp.float32)
    collision_k = jnp.asarray(build_collision(), jnp.float32)
    highest = lax.Precision.HIGHEST
    fluid_density = lax.optimization_barrier(jnp.sum(pops, axis=0))
    momentum = jnp.einsum('ci,i...->c...', table, pops, precision=highest)
    velocity = momentum / fluid_density
    projected = jnp.einsum('ci,c...->i...', table, velocity, precision=highest)
    speed_sq = lax.optimization_barrier(jnp.sum(velocity * velocity, axis=0))
    equilibrium = lattice_weights * fluid_density * (1.0 + 3.0 * projected + 4.5 * projected * projected - 1.5 * speed_sq)
    relaxed = pops - jnp.einsum('ij,j...->i...', collision_k, pops - equilibrium, precision=highest)
    grad_sq = lax.optimization_barrier(jnp.sum(grad * grad, axis=0))
    clipped_values = jnp.maximum(jnp.sqrt(grad_sq), GRAD_FLOOR)
    aligned_component = jnp.einsum('ci,c...->i...', table, grad, precision=highest)
    surface_perturbation = relaxed + 0.5 * SURFACE_COEF * (lattice_weights * aligned_component * aligned_component - balance * grad_sq) / clipped_values
    red_fraction = 0.5 * (1.0 + phase)
    separated_colours = red_fraction * surface_perturbation + SEGREGATION_RATE * 0.25 * fluid_density * (1.0 - phase * phase) * lattice_weights * aligned_component / clipped_values
    reflected_populations = pops[np.array(OPPOSITE)]
    total_post = jnp.where(wall_nodes, reflected_populations, surface_perturbation)
    red_after_collide = jnp.where(wall_nodes, red_fraction * reflected_populations, separated_colours)
    return (total_post, red_after_collide)

def move(field, ex, ey, ez):
    field = jnp.roll(field, ex, axis=0)
    zeros_row = jnp.zeros((field.shape[0], 1, field.shape[2]), jnp.float32)
    if ey == 1:
        field = jnp.concatenate([zeros_row, field[:, :-1]], axis=1)
    if ey == -1:
        field = jnp.concatenate([field[:, 1:], zeros_row], axis=1)
    return jnp.roll(field, ez, axis=2)

def reference(populations, labels, solid_mask):
    phase = jnp.where(labels > 0, 1.0, -1.0).astype(jnp.float32)
    ypos = jnp.arange(NY)
    wall = (ypos == 0) | (ypos == NY - 1)
    wall_nodes = (solid_mask > 0) | wall[None, :, None]
    pops = populations
    for step in range(STEPS):
        padded = jnp.concatenate([phase[-1:], phase, phase[:1]], axis=0)
        padded = jnp.pad(padded, ((0, 0), (1, 1), (0, 0)))
        grad = gradient_of(padded, NX, NY)

        def plane(position):
            plane_pops = lax.dynamic_index_in_dim(pops, position, 1, keepdims=False)
            plane_grad = lax.dynamic_index_in_dim(grad, position, 1, keepdims=False)
            plane_phase = lax.dynamic_index_in_dim(phase, position, 0, keepdims=False)
            plane_solid = lax.dynamic_index_in_dim(wall_nodes, position, 0, keepdims=False)
            return collide(plane_pops, plane_phase, plane_grad, plane_solid)
        total_post, red_after_collide = lax.map(plane, jnp.arange(NX))
        new_total = jnp.stack([move(total_post[:, d], *VELOCITY_SET[d]) for d in range(19)])
        new_red = jnp.stack([move(red_after_collide[:, d], *VELOCITY_SET[d]) for d in range(19)])
        pops = new_total
        phase = 2.0 * lax.optimization_barrier(jnp.sum(new_red, axis=0)) / lax.optimization_barrier(jnp.sum(new_total, axis=0)) - 1.0
    return (pops, phase)
```

```python
import functools

import jax
import jax.numpy as jnp
from jax import lax
from jax.experimental import pallas as pl
from jax.experimental.pallas import tpu as pltpu
from jax.sharding import PartitionSpec as P

E = [
    (0, 0, 0), (1, 0, 0), (-1, 0, 0), (0, 1, 0), (0, -1, 0), (0, 0, 1), (0, 0, -1),
    (1, 1, 0), (-1, -1, 0), (1, -1, 0), (-1, 1, 0), (1, 0, 1), (-1, 0, -1), (1, 0, -1),
    (-1, 0, 1), (0, 1, 1), (0, -1, -1), (0, 1, -1), (0, -1, 1),
]
OPP = [0, 2, 1, 4, 3, 6, 5, 8, 7, 10, 9, 12, 11, 14, 13, 16, 15, 18, 17]
ORDER = [
    9, (1, -1), 1, 11, 13, (1, 0), 7, (1, 1),
    3, 15, 17, (0, 1), 10, (-1, 1),
    2, 12, 14, (-1, 0), 8, (-1, -1),
    4, 16, 18, (0, -1),
    0, 5, 6, (0, 0),
]
SLOT = {key: place for place, key in enumerate(ORDER)}
RED = [key for key in ORDER if isinstance(key, tuple)]
NS = len(ORDER)
PAD = 8
MESH = pl.DeviceIdType.MESH


def relax(f):
    def plane(pp, mm, pm, mp):
        s1, d1, s2, d2 = f[pp] + f[mm], f[pp] - f[mm], f[pm] + f[mp], f[pm] - f[mp]
        return s1 + s2, s1 - s2, d1 + d2, d1 - d2

    xy = plane(7, 8, 9, 10)
    xz = plane(11, 12, 13, 14)
    yz = plane(15, 16, 17, 18)
    sx, sy, sz = f[1] + f[2], f[3] + f[4], f[5] + f[6]
    rho = (f[0] + sx) + (sy + sz) + ((xy[0] + xz[0]) + yz[0])
    jx = (f[1] - f[2]) + (xy[2] + xz[2])
    jy = (f[3] - f[4]) + (xy[3] + yz[2])
    jz = (f[5] - f[6]) + (xz[3] + yz[3])
    inv = 1.0 / rho
    ux, uy, uz = jx * inv, jy * inv, jz * inv
    qx, qy, qz = jx * ux, jy * uy, jz * uz
    third = rho * (1.0 / 3.0)
    dxx = (sx + (xy[0] + xz[0])) - (third + qx)
    dyy = (sy + (xy[0] + yz[0])) - (third + qy)
    dzz = (sz + (xz[0] + yz[0])) - (third + qz)
    trace = (dxx + dyy) + dzz
    part = trace * (1.0 / 12.0)
    base = (third + ((qx + qy) + qz)) * (1.0 / 3.0)
    base = rho * (1.0 / 9.0) + ((qx + qy) + qz) * (1.0 / 3.0)
    tx, ty, tz = jx * (1.0 / 3.0), jy * (1.0 / 3.0), jz * (1.0 / 3.0)
    out = list(f)

    def edges(moments, rest, cross, ta, tb, pp, mm, pm, mp):
        four = (moments[0] - base) + 0.5 * rest
        a = 0.35 * four
        d = 0.3125 * (moments[1] - cross)
        b = 0.3 * (moments[2] - ta)
        c = 0.3 * (moments[3] - tb)
        p1, p2, q1, q2 = a + d, a - d, b + c, b - c
        out[pp] = f[pp] - (p1 + q1)
        out[mm] = f[mm] - (p1 - q1)
        out[pm] = f[pm] - (p2 + q2)
        out[mp] = f[mp] - (p2 - q2)
        return a, b, c

    axy, bxy, cxy = edges(xy, qz, jx * uy, tx, ty, 7, 8, 9, 10)
    axz, bxz, cxz = edges(xz, qy, jx * uz, tx, tz, 11, 12, 13, 14)
    ayz, byz, cyz = edges(yz, qx, jy * uz, ty, tz, 15, 16, 17, 18)

    def faces(delta, a, b, plus, minus):
        half = (0.625 * delta - 0.5 * part) - 2.0 * a
        diff = 2.0 * b
        out[plus] = f[plus] - (half - diff)
        out[minus] = f[minus] - (half + diff)

    faces(dxx, axy + axz, bxy + bxz, 1, 2)
    faces(dyy, axy + ayz, cxy + byz, 3, 4)
    faces(dzz, axz + ayz, cxz + cyz, 5, 6)
    out[0] = f[0] + (trace - 4.0 * ((axy + axz) + ayz))
    return out, rho


def kernel(nx, ny, pops_ref, labels_ref, mask_ref, out_ref, phase_ref,
           f0, f1, p0, p1, rho_ref, send_sem, recv_sem):
    lx, ly, lz = labels_ref.shape
    rt = ly // 8
    top = PAD + ly
    gx, gy = lax.axis_index("gx"), lax.axis_index("gy")
    xp, xm = lax.rem(gx + 1, nx), lax.rem(gx + nx - 1, nx)
    up, down = gy < ny - 1, gy > 0

    barrier = pltpu.get_barrier_semaphore()

    def greet(ax, ay):
        pl.semaphore_signal(barrier, inc=1, device_id=(ax, ay), device_id_type=MESH)

    greet(xp, gy)
    greet(xm, gy)
    for flag, ay in ((up, gy + 1), (down, gy - 1)):
        @pl.when(flag)
        def _():
            greet(gx, ay)
            greet(xp, ay)
            greet(xm, ay)

    def move(ref, src, dst, k, ax, ay):
        return pltpu.make_async_remote_copy(
            src_ref=ref.at[src], dst_ref=ref.at[dst],
            send_sem=send_sem.at[k], recv_sem=recv_sem.at[k],
            device_id=(ax, ay), device_id_type=MESH)

    mid = pl.ds(PAD, ly)
    last, ghost_low = pl.ds(top - 8, 8), pl.ds(0, 8)
    first, ghost_high = pl.ds(PAD, 8), pl.ds(top, 8)
    own = pl.ds(1, lx)

    def phase_messages(ref, k):
        return [
            ("x", move(ref, (lx, mid), (0, mid), k, xp, gy), None, None),
            ("x", move(ref, (1, mid), (lx + 1, mid), k + 1, xm, gy), None, None),
            ("y", move(ref, (own, last), (own, ghost_low), k + 2, gx, gy + 1), up, down),
            ("y", move(ref, (own, first), (own, ghost_high), k + 3, gx, gy - 1), down, up),
            ("x", move(ref, (lx, last), (0, ghost_low), k + 4, xp, gy + 1), up, down),
            ("x", move(ref, (1, last), (lx + 1, ghost_low), k + 5, xm, gy + 1), up, down),
            ("x", move(ref, (lx, first), (0, ghost_high), k + 6, xp, gy - 1), down, up),
            ("x", move(ref, (1, first), (lx + 1, ghost_high), k + 7, xm, gy - 1), down, up),
        ]

    def field_messages(ref, k):
        def s(a, b):
            return pl.ds(a, b - a)

        return [
            ("x", move(ref, (lx, s(0, 8), mid), (0, s(0, 8), mid), k, xp, gy), None, None),
            ("x", move(ref, (1, s(12, 20), mid), (lx + 1, s(12, 20), mid), k + 1, xm, gy),
             None, None),
            ("x", move(ref, (lx, s(6, 8), last), (0, s(6, 8), ghost_low), k + 2, xp, gy + 1),
             up, down),
            ("x", move(ref, (1, s(12, 14), last), (lx + 1, s(12, 14), ghost_low), k + 3, xm,
                       gy + 1), up, down),
            ("x", move(ref, (lx, s(0, 2), first), (0, s(0, 2), ghost_high), k + 4, xp, gy - 1),
             down, up),
            ("x", move(ref, (1, s(18, 20), first), (lx + 1, s(18, 20), ghost_high), k + 5, xm,
                       gy - 1), down, up),
            ("y", move(ref, (own, s(6, 14), last), (own, s(6, 14), ghost_low), k + 6, gx, gy + 1),
             up, down),
            ("y", move(ref, (own, s(18, 24), first), (own, s(18, 24), ghost_high), k + 7, gx,
                       gy - 1), down, up),
            ("y", move(ref, (own, s(0, 2), first), (own, s(0, 2), ghost_high), k + 8, gx, gy - 1),
             down, up),
        ]

    def each(messages, kind, action):
        for name, copy, sends, receives in messages:
            if kind is not None and name != kind:
                continue
            flag = receives if action == "wait_recv" else sends
            if flag is None:
                getattr(copy, action)()
            else:
                pl.when(flag)(getattr(copy, action))

    pm0, fm0 = phase_messages(p0, 0), field_messages(f0, 8)
    pm1, fm1 = phase_messages(p1, 17), field_messages(f1, 25)

    def loop(kind, body):
        count = {"edge": 2, "inner": lx - 2, "all": lx}[kind]

        def step(t, carry):
            plane, row = t // rt, lax.rem(t, rt)
            if kind == "edge":
                plane = plane * (lx - 1)
            elif kind == "inner":
                plane = plane + 1
            body(plane, pl.multiple_of(row * 8, 8))
            return carry

        lax.fori_loop(0, count * rt, step, 0)

    for x in range(lx):
        p0[1 + x, PAD:top] = jnp.where(labels_ref[x] > 0, 1.0, -1.0).astype(jnp.float32)
    zero = jnp.zeros((8, lz), jnp.float32)

    def rim(flag, slots, rows):
        @pl.when(jnp.logical_not(flag))
        def _():
            for ref in (p0, p1):
                for x in range(lx + 2):
                    ref[x, rows] = zero
            for ref in (f0, f1):
                def fill(x, carry):
                    for s in slots:
                        ref[x, s, rows] = zero
                    return carry
                lax.fori_loop(0, lx + 2, fill, 0)

    rim(down, list(range(6, 14)), slice(0, 8))
    rim(up, list(range(18, 24)) + [0, 1], slice(top, top + 8))

    pl.semaphore_wait(barrier, 2 + 3 * (up.astype(jnp.int32) + down.astype(jnp.int32)))
    each(pm0, None, "start")

    def solid_at(x, r):
        rows = gy * ly + r + lax.broadcasted_iota(jnp.int32, (8, lz), 0)
        return (mask_ref[x, pl.ds(r, 8)] > 0) | (rows == 0) | (rows == ny * ly - 1)

    def collide(ref, x, r, f):
        solid = solid_at(x, r)
        relaxed, rho = relax(f)
        rho_ref[x, pl.ds(r, 8)] = rho
        for i in range(19):
            ref[x + 1, SLOT[i], pl.ds(PAD + r, 8)] = jnp.where(solid, f[OPP[i]], relaxed[i])

    def colour(ref, pref, x, r):
        at = pl.ds(PAD + r, 8)
        up_r, dn_r = pl.ds(PAD + 1 + r, 8), pl.ds(PAD - 1 + r, 8)
        p = pref[x + 1, at]
        e, w = pref[x + 2, at], pref[x, at]
        n, s = pref[x + 1, up_r], pref[x + 1, dn_r]
        ne, se = pref[x + 2, up_r], pref[x + 2, dn_r]
        nw, sw = pref[x, up_r], pref[x, dn_r]

        def zsum(v):
            return pltpu.roll(v, 1, 1) + pltpu.roll(v, lz - 1, 1)

        dx, dy = e - w, n - s
        around = (e + w) + (n + s) + 2.0 * p
        ca, cb = ne - sw, se - nw
        twelfth = 1.0 / 12.0
        hx = (2.0 * dx + zsum(dx) + (ca + cb)) * twelfth
        hy = (2.0 * dy + zsum(dy) + (ca - cb)) * twelfth
        hz = (pltpu.roll(around, lz - 1, 1) - pltpu.roll(around, 1, 1)) * twelfth
        xx, yy, zz = hx * hx, hy * hy, hz * hz
        g2 = (xx + yy) + zz
        inv = lax.rsqrt(jnp.maximum(g2, 0.01))
        inv = jnp.where(solid_at(x, r), 0.0, inv)
        rho = rho_ref[x, pl.ds(r, 8)]
        c18 = (0.1 / 18.0) * inv
        c36 = 0.5 * c18
        k18 = (0.175 / 18.0) * (rho * (1.0 - p * p)) * inv
        k36 = 0.5 * k18
        red = 0.5 + 0.5 * p
        total, reds = {}, {}

        def read(i):
            return ref[x + 1, SLOT[i], at]

        def pair(plus, minus, square, k, along):
            shift = k * along
            for i, sign in ((plus, 1), (minus, -1)):
                value = read(i) + square
                total[i] = value
                reds[i] = red * value + shift if sign > 0 else red * value - shift

        total[0] = read(0) + (6.0 * c18) * g2
        reds[0] = red * total[0]
        pair(1, 2, c18 * (xx - g2), k18, hx)
        pair(3, 4, c18 * (yy - g2), k18, hy)
        pair(5, 6, c18 * (zz - g2), k18, hz)
        for plus, minus, along in ((7, 8, hx + hy), (9, 10, hx - hy), (11, 12, hx + hz),
                                   (13, 14, hx - hz), (15, 16, hy + hz), (17, 18, hy - hz)):
            pair(plus, minus, c36 * (along * along - g2), k36, along)
        sums = {}
        for i, (ex, ey, ez) in enumerate(E):
            value, part = total[i], reds[i]
            if ez != 0:
                value = pltpu.roll(value, ez % lz, 1)
                part = pltpu.roll(part, ez % lz, 1)
            ref[x + 1, SLOT[i], at] = value
            sums[(ex, ey)] = sums[(ex, ey)] + part if (ex, ey) in sums else part
        for key, value in sums.items():
            ref[x + 1, SLOT[key], at] = value

    def pull(ref, x, r, key, ex, ey):
        return ref[x + 1 - ex, SLOT[key], pl.ds(PAD - ey + r, 8)]

    def arrive(ref, x, r):
        return [pull(ref, x, r, i, e[0], e[1]) for i, e in enumerate(E)]

    def tree(values):
        while len(values) > 1:
            values = [sum(values[i:i + 2]) for i in range(0, len(values), 2)]
        return values[0]

    def mix(ref, x, r, f):
        red = tree([pull(ref, x, r, key, *key) for key in RED])
        return 2.0 * red / tree(list(f)) - 1.0

    loop("all", lambda x, r: collide(f0, x, r, [pops_ref[i, x, pl.ds(r, 8)] for i in range(19)]))
    each(pm0, None, "wait_recv")
    loop("edge", functools.partial(colour, f0, p0))
    each(fm0, "x", "start")
    loop("inner", functools.partial(colour, f0, p0))
    each(fm0, "y", "start")
    each(fm0, "y", "wait_recv")

    def inner(x, r):
        f = arrive(f0, x, r)
        p1[x + 1, pl.ds(PAD + r, 8)] = mix(f0, x, r, f)
        collide(f1, x, r, f)

    loop("inner", inner)
    each(fm0, "x", "wait_recv")

    def edge_phase(x, r):
        p1[x + 1, pl.ds(PAD + r, 8)] = mix(f0, x, r, arrive(f0, x, r))

    loop("edge", edge_phase)
    each(pm1, None, "start")
    loop("edge", lambda x, r: collide(f1, x, r, arrive(f0, x, r)))
    each(pm1, None, "wait_recv")
    loop("edge", functools.partial(colour, f1, p1))
    each(fm1, "x", "start")
    loop("inner", functools.partial(colour, f1, p1))
    each(fm1, "y", "start")
    each(fm1, "y", "wait_recv")

    def finish(x, r):
        f = arrive(f1, x, r)
        for i in range(19):
            out_ref[i, x, pl.ds(r, 8)] = f[i]
        phase_ref[x, pl.ds(r, 8)] = mix(f1, x, r, f)

    loop("inner", finish)
    each(fm1, "x", "wait_recv")
    loop("edge", finish)
    for messages in (pm0, fm0, pm1, fm1):
        each(messages, None, "wait_send")


def solution(mesh):
    nx, ny = mesh.shape["gx"], mesh.shape["gy"]

    def on_device(populations, labels, solid_mask):
        lx, ly, lz = labels.shape
        rows = ly + 2 * PAD
        return pl.pallas_call(
            functools.partial(kernel, nx, ny),
            out_shape=(jax.ShapeDtypeStruct((19, lx, ly, lz), jnp.float32),
                       jax.ShapeDtypeStruct((lx, ly, lz), jnp.float32)),
            in_specs=[pl.BlockSpec(memory_space=pltpu.VMEM)] * 3,
            out_specs=(pl.BlockSpec(memory_space=pltpu.VMEM),) * 2,
            scratch_shapes=[
                pltpu.VMEM((lx + 2, NS, rows, lz), jnp.float32),
                pltpu.VMEM((lx + 2, NS, rows, lz), jnp.float32),
                pltpu.VMEM((lx + 2, rows, lz), jnp.float32),
                pltpu.VMEM((lx + 2, rows, lz), jnp.float32),
                pltpu.VMEM((lx, ly, lz), jnp.float32),
                pltpu.SemaphoreType.DMA((34,)),
                pltpu.SemaphoreType.DMA((34,)),
            ],
            compiler_params=pltpu.CompilerParams(
                collective_id=0, has_side_effects=True, vmem_limit_bytes=40 * 2**20),
        )(populations, labels, solid_mask)

    return jax.shard_map(
        on_device, mesh=mesh,
        in_specs=(P(None, "gx", "gy", None), P("gx", "gy", None), P("gx", "gy", None)),
        out_specs=(P(None, "gx", "gy", None), P("gx", "gy", None)),
        check_vma=False)
```

```python
import functools

import jax
import jax.numpy as jnp
from jax import lax
from jax.experimental import pallas as pl
from jax.experimental.pallas import tpu as pltpu
from jax.sharding import PartitionSpec as P

E = [
    (0, 0, 0), (1, 0, 0), (-1, 0, 0), (0, 1, 0), (0, -1, 0), (0, 0, 1), (0, 0, -1),
    (1, 1, 0), (-1, -1, 0), (1, -1, 0), (-1, 1, 0), (1, 0, 1), (-1, 0, -1), (1, 0, -1),
    (-1, 0, 1), (0, 1, 1), (0, -1, -1), (0, 1, -1), (0, -1, 1),
]
OPP = [0, 2, 1, 4, 3, 6, 5, 8, 7, 10, 9, 12, 11, 14, 13, 16, 15, 18, 17]
ORDER = [
    9, (1, -1), 1, 11, 13, (1, 0), 7, (1, 1),
    3, 15, 17, (0, 1), 10, (-1, 1),
    2, 12, 14, (-1, 0), 8, (-1, -1),
    4, 16, 18, (0, -1),
    0, 5, 6, (0, 0),
]
SLOT = {key: place for place, key in enumerate(ORDER)}
RED = [key for key in ORDER if isinstance(key, tuple)]
NS = len(ORDER)
PAD = 8
MESH = pl.DeviceIdType.MESH


def relax(f):
    def plane(pp, mm, pm, mp):
        s1, d1, s2, d2 = f[pp] + f[mm], f[pp] - f[mm], f[pm] + f[mp], f[pm] - f[mp]
        return s1 + s2, s1 - s2, d1 + d2, d1 - d2

    xy = plane(7, 8, 9, 10)
    xz = plane(11, 12, 13, 14)
    yz = plane(15, 16, 17, 18)
    sx, sy, sz = f[1] + f[2], f[3] + f[4], f[5] + f[6]
    rho = (f[0] + sx) + (sy + sz) + ((xy[0] + xz[0]) + yz[0])
    jx = (f[1] - f[2]) + (xy[2] + xz[2])
    jy = (f[3] - f[4]) + (xy[3] + yz[2])
    jz = (f[5] - f[6]) + (xz[3] + yz[3])
    inv = 1.0 / rho
    ux, uy, uz = jx * inv, jy * inv, jz * inv
    qx, qy, qz = jx * ux, jy * uy, jz * uz
    third = rho * (1.0 / 3.0)
    dxx = (sx + (xy[0] + xz[0])) - (third + qx)
    dyy = (sy + (xy[0] + yz[0])) - (third + qy)
    dzz = (sz + (xz[0] + yz[0])) - (third + qz)
    trace = (dxx + dyy) + dzz
    part = trace * (1.0 / 12.0)
    base = rho * (1.0 / 9.0) + ((qx + qy) + qz) * (1.0 / 3.0)
    tx, ty, tz = jx * (1.0 / 3.0), jy * (1.0 / 3.0), jz * (1.0 / 3.0)
    out = list(f)

    def edges(moments, rest, cross, ta, tb, pp, mm, pm, mp):
        four = (moments[0] - base) + 0.5 * rest
        a = 0.35 * four
        d = 0.3125 * (moments[1] - cross)
        b = 0.3 * (moments[2] - ta)
        c = 0.3 * (moments[3] - tb)
        p1, p2, q1, q2 = a + d, a - d, b + c, b - c
        out[pp] = f[pp] - (p1 + q1)
        out[mm] = f[mm] - (p1 - q1)
        out[pm] = f[pm] - (p2 + q2)
        out[mp] = f[mp] - (p2 - q2)
        return a, b, c

    axy, bxy, cxy = edges(xy, qz, jx * uy, tx, ty, 7, 8, 9, 10)
    axz, bxz, cxz = edges(xz, qy, jx * uz, tx, tz, 11, 12, 13, 14)
    ayz, byz, cyz = edges(yz, qx, jy * uz, ty, tz, 15, 16, 17, 18)

    def faces(delta, a, b, plus, minus):
        half = (0.625 * delta - 0.5 * part) - 2.0 * a
        diff = 2.0 * b
        out[plus] = f[plus] - (half - diff)
        out[minus] = f[minus] - (half + diff)

    faces(dxx, axy + axz, bxy + bxz, 1, 2)
    faces(dyy, axy + ayz, cxy + byz, 3, 4)
    faces(dzz, axz + ayz, cxz + cyz, 5, 6)
    out[0] = f[0] + (trace - 4.0 * ((axy + axz) + ayz))
    return out, rho


def kernel(nx, ny, pops_hbm, labels_hbm, mask_hbm, out_ref, phase_ref,
           f0, f1, p0, p1, rho_ref, pops_ref, labels_ref, mask_ref, load_sem,
           send_sem, recv_sem):
    lx, ly, lz = labels_ref.shape
    tr = 16 if ly % 16 == 0 else 8
    rt = ly // tr
    top = PAD + ly
    gx, gy = lax.axis_index("gx"), lax.axis_index("gy")
    xp, xm = lax.rem(gx + 1, nx), lax.rem(gx + nx - 1, nx)
    up, down = gy < ny - 1, gy > 0

    barrier = pltpu.get_barrier_semaphore()

    def greet(ax, ay):
        pl.semaphore_signal(barrier, inc=1, device_id=(ax, ay), device_id_type=MESH)

    greet(xp, gy)
    greet(xm, gy)
    for flag, ay in ((up, gy + 1), (down, gy - 1)):
        @pl.when(flag)
        def _():
            greet(gx, ay)
            greet(xp, ay)
            greet(xm, ay)

    def load_plane(x):
        return pltpu.make_async_copy(pops_hbm.at[:, x], pops_ref.at[:, x], load_sem.at[x])

    load_labels = pltpu.make_async_copy(labels_hbm, labels_ref, load_sem.at[lx])
    load_mask = pltpu.make_async_copy(mask_hbm, mask_ref, load_sem.at[lx + 1])
    load_labels.start()
    for x in range(lx):
        load_plane(x).start()
        if x == 0:
            load_mask.start()

    def move(ref, src, dst, k, ax, ay):
        return pltpu.make_async_remote_copy(
            src_ref=ref.at[src], dst_ref=ref.at[dst],
            send_sem=send_sem.at[k], recv_sem=recv_sem.at[k],
            device_id=(ax, ay), device_id_type=MESH)

    mid = pl.ds(PAD, ly)
    last, ghost_low = pl.ds(top - 8, 8), pl.ds(0, 8)
    first, ghost_high = pl.ds(PAD, 8), pl.ds(top, 8)
    own = pl.ds(1, lx)

    def phase_messages(ref, k):
        return [
            ("x", move(ref, (lx, mid), (0, mid), k, xp, gy), None, None),
            ("x", move(ref, (1, mid), (lx + 1, mid), k + 1, xm, gy), None, None),
            ("y", move(ref, (own, last), (own, ghost_low), k + 2, gx, gy + 1), up, down),
            ("y", move(ref, (own, first), (own, ghost_high), k + 3, gx, gy - 1), down, up),
            ("x", move(ref, (lx, last), (0, ghost_low), k + 4, xp, gy + 1), up, down),
            ("x", move(ref, (1, last), (lx + 1, ghost_low), k + 5, xm, gy + 1), up, down),
            ("x", move(ref, (lx, first), (0, ghost_high), k + 6, xp, gy - 1), down, up),
            ("x", move(ref, (1, first), (lx + 1, ghost_high), k + 7, xm, gy - 1), down, up),
        ]

    def field_messages(ref, k):
        def s(a, b):
            return pl.ds(a, b - a)

        return [
            ("x", move(ref, (lx, s(0, 8), mid), (0, s(0, 8), mid), k, xp, gy), None, None),
            ("x", move(ref, (1, s(12, 20), mid), (lx + 1, s(12, 20), mid), k + 1, xm, gy),
             None, None),
            ("x", move(ref, (lx, s(6, 8), last), (0, s(6, 8), ghost_low), k + 2, xp, gy + 1),
             up, down),
            ("x", move(ref, (1, s(12, 14), last), (lx + 1, s(12, 14), ghost_low), k + 3, xm,
                       gy + 1), up, down),
            ("x", move(ref, (lx, s(0, 2), first), (0, s(0, 2), ghost_high), k + 4, xp, gy - 1),
             down, up),
            ("x", move(ref, (1, s(18, 20), first), (lx + 1, s(18, 20), ghost_high), k + 5, xm,
                       gy - 1), down, up),
            ("y", move(ref, (own, s(6, 14), last), (own, s(6, 14), ghost_low), k + 6, gx, gy + 1),
             up, down),
            ("y", move(ref, (own, s(18, 24), first), (own, s(18, 24), ghost_high), k + 7, gx,
                       gy - 1), down, up),
            ("y", move(ref, (own, s(0, 2), first), (own, s(0, 2), ghost_high), k + 8, gx, gy - 1),
             down, up),
        ]

    def each(messages, kind, action):
        for name, copy, sends, receives in messages:
            if kind is not None and name != kind:
                continue
            flag = receives if action == "wait_recv" else sends
            if flag is None:
                getattr(copy, action)()
            else:
                pl.when(flag)(getattr(copy, action))

    pm0, fm0 = phase_messages(p0, 0), field_messages(f0, 8)
    pm1, fm1 = phase_messages(p1, 17), field_messages(f1, 25)

    def loop(kind, body):
        count = {"edge": 2, "inner": lx - 2, "all": lx}[kind]

        def step(t, carry):
            plane, row = t // rt, lax.rem(t, rt)
            if kind == "edge":
                plane = plane * (lx - 1)
            elif kind == "inner":
                plane = plane + 1
            body(plane, pl.multiple_of(row * tr, 8))
            return carry

        lax.fori_loop(0, count * rt, step, 0)

    zero = jnp.zeros((8, lz), jnp.float32)

    def rim(flag, slots, rows):
        @pl.when(jnp.logical_not(flag))
        def _():
            for ref in (p0, p1):
                for x in range(lx + 2):
                    ref[x, rows] = zero
            for ref in (f0, f1):
                def fill(x, carry):
                    for s in slots:
                        ref[x, s, rows] = zero
                    return carry
                lax.fori_loop(0, lx + 2, fill, 0)

    rim(down, list(range(6, 14)), slice(0, 8))
    rim(up, list(range(18, 24)) + [0, 1], slice(top, top + 8))

    load_labels.wait()
    for x in range(lx):
        p0[1 + x, PAD:top] = jnp.where(labels_ref[x] > 0, 1.0, -1.0).astype(jnp.float32)
    pl.semaphore_wait(barrier, 2 + 3 * (up.astype(jnp.int32) + down.astype(jnp.int32)))
    each(pm0, None, "start")

    def solid_at(x, r):
        rows = gy * ly + r + lax.broadcasted_iota(jnp.int32, (tr, lz), 0)
        return (mask_ref[x, pl.ds(r, tr)] > 0) | (rows == 0) | (rows == ny * ly - 1)

    def collide(ref, x, r, f):
        solid = solid_at(x, r)
        relaxed, rho = relax(f)
        rho_ref[x, pl.ds(r, tr)] = rho
        for i in range(19):
            ref[x + 1, SLOT[i], pl.ds(PAD + r, tr)] = jnp.where(solid, f[OPP[i]], relaxed[i])

    def colour(ref, pref, x, r):
        at = pl.ds(PAD + r, tr)
        up_r, dn_r = pl.ds(PAD + 1 + r, tr), pl.ds(PAD - 1 + r, tr)
        p = pref[x + 1, at]
        e, w = pref[x + 2, at], pref[x, at]
        n, s = pref[x + 1, up_r], pref[x + 1, dn_r]
        ne, se = pref[x + 2, up_r], pref[x + 2, dn_r]
        nw, sw = pref[x, up_r], pref[x, dn_r]

        def zsum(v):
            return pltpu.roll(v, 1, 1) + pltpu.roll(v, lz - 1, 1)

        dx, dy = e - w, n - s
        around = (e + w) + (n + s) + 2.0 * p
        ca, cb = ne - sw, se - nw
        twelfth = 1.0 / 12.0
        hx = (2.0 * dx + zsum(dx) + (ca + cb)) * twelfth
        hy = (2.0 * dy + zsum(dy) + (ca - cb)) * twelfth
        hz = (pltpu.roll(around, lz - 1, 1) - pltpu.roll(around, 1, 1)) * twelfth
        xx, yy, zz = hx * hx, hy * hy, hz * hz
        g2 = (xx + yy) + zz
        inv = lax.rsqrt(jnp.maximum(g2, 0.01))
        inv = jnp.where(solid_at(x, r), 0.0, inv)
        rho = rho_ref[x, pl.ds(r, tr)]
        c18 = (0.1 / 18.0) * inv
        c36 = 0.5 * c18
        k18 = (0.175 / 18.0) * (rho * (1.0 - p * p)) * inv
        k36 = 0.5 * k18
        red = 0.5 + 0.5 * p
        total, reds = {}, {}

        def read(i):
            return ref[x + 1, SLOT[i], at]

        def pair(plus, minus, square, k, along):
            shift = k * along
            for i, sign in ((plus, 1), (minus, -1)):
                value = read(i) + square
                total[i] = value
                reds[i] = red * value + shift if sign > 0 else red * value - shift

        total[0] = read(0) + (6.0 * c18) * g2
        reds[0] = red * total[0]
        pair(1, 2, c18 * (xx - g2), k18, hx)
        pair(3, 4, c18 * (yy - g2), k18, hy)
        pair(5, 6, c18 * (zz - g2), k18, hz)
        for plus, minus, along in ((7, 8, hx + hy), (9, 10, hx - hy), (11, 12, hx + hz),
                                   (13, 14, hx - hz), (15, 16, hy + hz), (17, 18, hy - hz)):
            pair(plus, minus, c36 * (along * along - g2), k36, along)
        sums = {}
        for i, (ex, ey, ez) in enumerate(E):
            value, part = total[i], reds[i]
            if ez != 0:
                value = pltpu.roll(value, ez % lz, 1)
                part = pltpu.roll(part, ez % lz, 1)
            ref[x + 1, SLOT[i], at] = value
            sums[(ex, ey)] = sums[(ex, ey)] + part if (ex, ey) in sums else part
        for key, value in sums.items():
            ref[x + 1, SLOT[key], at] = value

    def pull(ref, x, r, key, ex, ey):
        return ref[x + 1 - ex, SLOT[key], pl.ds(PAD - ey + r, tr)]

    def arrive(ref, x, r):
        return [pull(ref, x, r, i, e[0], e[1]) for i, e in enumerate(E)]

    def tree(values):
        while len(values) > 1:
            values = [sum(values[i:i + 2]) for i in range(0, len(values), 2)]
        return values[0]

    def mix(ref, x, r, f):
        red = tree([pull(ref, x, r, key, *key) for key in RED])
        return 2.0 * red / tree(list(f)) - 1.0

    load_mask.wait()

    def first_plane(x, carry):
        load_plane(x).wait()

        def step(t, carry):
            r = pl.multiple_of(t * tr, 8)
            collide(f0, x, r, [pops_ref[i, x, pl.ds(r, tr)] for i in range(19)])
            return carry

        return lax.fori_loop(0, rt, step, carry)

    lax.fori_loop(0, lx, first_plane, 0)
    each(pm0, None, "wait_recv")
    loop("edge", functools.partial(colour, f0, p0))
    each(fm0, "x", "start")
    loop("inner", functools.partial(colour, f0, p0))
    each(fm0, "y", "start")
    each(fm0, "y", "wait_recv")

    def inner(x, r):
        f = arrive(f0, x, r)
        p1[x + 1, pl.ds(PAD + r, tr)] = mix(f0, x, r, f)
        collide(f1, x, r, f)

    loop("inner", inner)
    each(fm0, "x", "wait_recv")

    def edge_phase(x, r):
        p1[x + 1, pl.ds(PAD + r, tr)] = mix(f0, x, r, arrive(f0, x, r))

    loop("edge", edge_phase)
    each(pm1, None, "start")
    loop("edge", lambda x, r: collide(f1, x, r, arrive(f0, x, r)))
    each(pm1, None, "wait_recv")
    loop("edge", functools.partial(colour, f1, p1))
    each(fm1, "x", "start")
    loop("inner", functools.partial(colour, f1, p1))
    each(fm1, "y", "start")
    each(fm1, "y", "wait_recv")

    def finish(x, r):
        f = arrive(f1, x, r)
        for i in range(19):
            out_ref[i, x, pl.ds(r, tr)] = f[i]
        phase_ref[x, pl.ds(r, tr)] = mix(f1, x, r, f)

    loop("inner", finish)
    each(fm1, "x", "wait_recv")
    loop("edge", finish)
    for messages in (pm0, fm0, pm1, fm1):
        each(messages, None, "wait_send")


def solution(mesh):
    nx, ny = mesh.shape["gx"], mesh.shape["gy"]

    def on_device(populations, labels, solid_mask):
        lx, ly, lz = labels.shape
        rows = ly + 2 * PAD
        return pl.pallas_call(
            functools.partial(kernel, nx, ny),
            out_shape=(jax.ShapeDtypeStruct((19, lx, ly, lz), jnp.float32),
                       jax.ShapeDtypeStruct((lx, ly, lz), jnp.float32)),
            in_specs=[pl.BlockSpec(memory_space=pltpu.HBM)] * 3,
            out_specs=(pl.BlockSpec(memory_space=pltpu.VMEM),) * 2,
            scratch_shapes=[
                pltpu.VMEM((lx + 2, NS, rows, lz), jnp.float32),
                pltpu.VMEM((lx + 2, NS, rows, lz), jnp.float32),
                pltpu.VMEM((lx + 2, rows, lz), jnp.float32),
                pltpu.VMEM((lx + 2, rows, lz), jnp.float32),
                pltpu.VMEM((lx, ly, lz), jnp.float32),
                pltpu.VMEM((19, lx, ly, lz), jnp.float32),
                pltpu.VMEM((lx, ly, lz), jnp.int32),
                pltpu.VMEM((lx, ly, lz), jnp.int32),
                pltpu.SemaphoreType.DMA((lx + 2,)),
                pltpu.SemaphoreType.DMA((34,)),
                pltpu.SemaphoreType.DMA((34,)),
            ],
            compiler_params=pltpu.CompilerParams(
                collective_id=0, has_side_effects=True, vmem_limit_bytes=40 * 2**20),
        )(populations, labels, solid_mask)

    return jax.shard_map(
        on_device, mesh=mesh,
        in_specs=(P(None, "gx", "gy", None), P("gx", "gy", None), P("gx", "gy", None)),
        out_specs=(P(None, "gx", "gy", None), P("gx", "gy", None)),
        check_vma=False)
```

```python
import functools

import jax
import jax.numpy as jnp
from jax import lax
from jax.experimental import pallas as pl
from jax.experimental.pallas import tpu as pltpu
from jax.sharding import PartitionSpec as P

E = [
    (0, 0, 0), (1, 0, 0), (-1, 0, 0), (0, 1, 0), (0, -1, 0), (0, 0, 1), (0, 0, -1),
    (1, 1, 0), (-1, -1, 0), (1, -1, 0), (-1, 1, 0), (1, 0, 1), (-1, 0, -1), (1, 0, -1),
    (-1, 0, 1), (0, 1, 1), (0, -1, -1), (0, 1, -1), (0, -1, 1),
]
OPP = [0, 2, 1, 4, 3, 6, 5, 8, 7, 10, 9, 12, 11, 14, 13, 16, 15, 18, 17]
ORDER = [
    (1, -1), 9, 1, 11, 13, (1, 0), 7, (1, 1),
    3, 15, 17, (0, 1), (-1, 1), 10,
    2, 12, 14, (-1, 0), 8, (-1, -1),
    4, 16, 18, (0, -1),
    0, 5, 6, (0, 0),
]
SLOT = {key: place for place, key in enumerate(ORDER)}
RED = [key for key in ORDER if isinstance(key, tuple)]
NS = len(ORDER)
PAD = 8
MESH = pl.DeviceIdType.MESH


def relax(f):
    def plane(pp, mm, pm, mp):
        s1, d1, s2, d2 = f[pp] + f[mm], f[pp] - f[mm], f[pm] + f[mp], f[pm] - f[mp]
        return s1 + s2, s1 - s2, d1 + d2, d1 - d2

    xy = plane(7, 8, 9, 10)
    xz = plane(11, 12, 13, 14)
    yz = plane(15, 16, 17, 18)
    sx, sy, sz = f[1] + f[2], f[3] + f[4], f[5] + f[6]
    rho = (f[0] + sx) + (sy + sz) + ((xy[0] + xz[0]) + yz[0])
    jx = (f[1] - f[2]) + (xy[2] + xz[2])
    jy = (f[3] - f[4]) + (xy[3] + yz[2])
    jz = (f[5] - f[6]) + (xz[3] + yz[3])
    inv = 1.0 / rho
    ux, uy, uz = jx * inv, jy * inv, jz * inv
    qx, qy, qz = jx * ux, jy * uy, jz * uz
    third = rho * (1.0 / 3.0)
    dxx = (sx + (xy[0] + xz[0])) - (third + qx)
    dyy = (sy + (xy[0] + yz[0])) - (third + qy)
    dzz = (sz + (xz[0] + yz[0])) - (third + qz)
    trace = (dxx + dyy) + dzz
    part = trace * (1.0 / 12.0)
    base = rho * (1.0 / 9.0) + ((qx + qy) + qz) * (1.0 / 3.0)
    tx, ty, tz = jx * (1.0 / 3.0), jy * (1.0 / 3.0), jz * (1.0 / 3.0)
    out = list(f)

    def edges(moments, rest, cross, ta, tb, pp, mm, pm, mp):
        four = (moments[0] - base) + 0.5 * rest
        a = 0.35 * four
        d = 0.3125 * (moments[1] - cross)
        b = 0.3 * (moments[2] - ta)
        c = 0.3 * (moments[3] - tb)
        p1, p2, q1, q2 = a + d, a - d, b + c, b - c
        out[pp] = f[pp] - (p1 + q1)
        out[mm] = f[mm] - (p1 - q1)
        out[pm] = f[pm] - (p2 + q2)
        out[mp] = f[mp] - (p2 - q2)
        return a, b, c

    axy, bxy, cxy = edges(xy, qz, jx * uy, tx, ty, 7, 8, 9, 10)
    axz, bxz, cxz = edges(xz, qy, jx * uz, tx, tz, 11, 12, 13, 14)
    ayz, byz, cyz = edges(yz, qx, jy * uz, ty, tz, 15, 16, 17, 18)

    def faces(delta, a, b, plus, minus):
        half = (0.625 * delta - 0.5 * part) - 2.0 * a
        diff = 2.0 * b
        out[plus] = f[plus] - (half - diff)
        out[minus] = f[minus] - (half + diff)

    faces(dxx, axy + axz, bxy + bxz, 1, 2)
    faces(dyy, axy + ayz, cxy + byz, 3, 4)
    faces(dzz, axz + ayz, cxz + cyz, 5, 6)
    out[0] = f[0] + (trace - 4.0 * ((axy + axz) + ayz))
    return out, rho


def kernel(nx, ny, pops_hbm, labels_hbm, mask_hbm, out_hbm, phase_hbm,
           f0, f1, p0, p1, rho_ref, pops_ref, labels_ref, mask_ref, y0, y1, load_sem,
           store_sem, send_sem, recv_sem):
    lx, ly, lz = labels_ref.shape
    tr = 16 if ly % 16 == 0 else 8
    rt = ly // tr
    top = PAD + ly
    gx, gy = lax.axis_index("gx"), lax.axis_index("gy")
    xp, xm = lax.rem(gx + 1, nx), lax.rem(gx + nx - 1, nx)
    up, down = gy < ny - 1, gy > 0

    barrier = pltpu.get_barrier_semaphore()

    def greet(ax, ay):
        pl.semaphore_signal(barrier, inc=1, device_id=(ax, ay), device_id_type=MESH)

    greet(xp, gy)
    greet(xm, gy)
    for flag, ay in ((up, gy + 1), (down, gy - 1)):
        @pl.when(flag)
        def _():
            greet(gx, ay)
            greet(xp, ay)
            greet(xm, ay)

    def load_plane(x):
        return pltpu.make_async_copy(pops_hbm.at[:, x], pops_ref.at[:, x], load_sem.at[x])

    load_labels = pltpu.make_async_copy(labels_hbm, labels_ref, load_sem.at[lx])
    load_mask = pltpu.make_async_copy(mask_hbm, mask_ref, load_sem.at[lx + 1])
    load_labels.start()
    for x in range(lx):
        load_plane(x).start()
        if x == 0:
            load_mask.start()

    def move(ref, src, dst, k, ax, ay):
        return pltpu.make_async_remote_copy(
            src_ref=ref.at[src], dst_ref=ref.at[dst],
            send_sem=send_sem.at[k], recv_sem=recv_sem.at[k],
            device_id=(ax, ay), device_id_type=MESH)

    mid = pl.ds(PAD, ly)
    last, ghost_low = pl.ds(top - 8, 8), pl.ds(0, 8)
    first, ghost_high = pl.ds(PAD, 8), pl.ds(top, 8)
    own = pl.ds(1, lx)

    def phase_messages(ref, k):
        return [
            ("x", move(ref, (lx, mid), (0, mid), k, xp, gy), None, None),
            ("x", move(ref, (1, mid), (lx + 1, mid), k + 1, xm, gy), None, None),
            ("y", move(ref, (own, last), (own, ghost_low), k + 2, gx, gy + 1), up, down),
            ("y", move(ref, (own, first), (own, ghost_high), k + 3, gx, gy - 1), down, up),
            ("x", move(ref, (lx, last), (0, ghost_low), k + 4, xp, gy + 1), up, down),
            ("x", move(ref, (1, last), (lx + 1, ghost_low), k + 5, xm, gy + 1), up, down),
            ("x", move(ref, (lx, first), (0, ghost_high), k + 6, xp, gy - 1), down, up),
            ("x", move(ref, (1, first), (lx + 1, ghost_high), k + 7, xm, gy - 1), down, up),
        ]

    def field_messages(ref, rows, k):
        def s(a, b):
            return pl.ds(a, b - a)

        return [
            ("x", move(ref, (lx, s(1, 7), mid), (0, s(1, 7), mid), k, xp, gy), None, None),
            ("x", move(ref, (1, s(13, 19), mid), (lx + 1, s(13, 19), mid), k + 1, xm, gy),
             None, None),
            ("x", move(ref, (lx, s(6, 8), last), (0, s(6, 8), ghost_low), k + 2, xp, gy + 1),
             up, down),
            ("x", move(ref, (1, s(12, 14), last), (lx + 1, s(12, 14), ghost_low), k + 3, xm,
                       gy + 1), up, down),
            ("x", move(ref, (lx, s(0, 2), first), (0, s(0, 2), ghost_high), k + 4, xp, gy - 1),
             down, up),
            ("x", move(ref, (1, s(18, 20), first), (lx + 1, s(18, 20), ghost_high), k + 5, xm,
                       gy - 1), down, up),
            ("y", move(rows, 0, 1, k + 6, gx, gy + 1), up, down),
            ("y", move(rows, 2, 3, k + 7, gx, gy - 1), down, up),
        ]

    upward = list(range(6, 14))
    downward = list(range(18, 24)) + [0, 1]

    def pack(ref, rows):
        for flag, slots, place, row in ((up, upward, 0, top - 1), (down, downward, 2, PAD)):
            @pl.when(flag)
            def _():
                for x in range(lx):
                    for k, slot in enumerate(slots):
                        rows[place, x, k:k + 1] = ref[x + 1, slot, row:row + 1]

    def unpack(ref, rows):
        for flag, slots, place, row in ((down, upward, 1, PAD - 1), (up, downward, 3, top)):
            @pl.when(flag)
            def _():
                for x in range(lx):
                    for k, slot in enumerate(slots):
                        ref[x + 1, slot, row:row + 1] = rows[place, x, k:k + 1]

    def gather_red(ref):
        for x, ex in ((lx, 1), (1, -1)):
            ref[x, SLOT[(ex, 0)], PAD:top] = (
                ref[x, SLOT[(ex, 0)], PAD:top] + ref[x, SLOT[(ex, 1)], PAD - 1:top - 1]
                + ref[x, SLOT[(ex, -1)], PAD + 1:top + 1])

    def each(messages, kind, action):
        for name, copy, sends, receives in messages:
            if kind is not None and name != kind:
                continue
            flag = receives if action == "wait_recv" else sends
            if flag is None:
                getattr(copy, action)()
            else:
                pl.when(flag)(getattr(copy, action))

    pm0, fm0 = phase_messages(p0, 0), field_messages(f0, y0, 8)
    pm1, fm1 = phase_messages(p1, 16), field_messages(f1, y1, 24)

    def loop(kind, body):
        count = {"edge": 2, "inner": lx - 2, "all": lx}[kind]

        def step(t, carry):
            plane, row = t // rt, lax.rem(t, rt)
            if kind == "edge":
                plane = plane * (lx - 1)
            elif kind == "inner":
                plane = plane + 1
            body(plane, pl.multiple_of(row * tr, 8))
            return carry

        lax.fori_loop(0, count * rt, step, 0)

    zero = jnp.zeros((8, lz), jnp.float32)

    def fill(x, carry):
        for ref in (f0, f1):
            for slot in upward:
                ref[x, slot, 0:8] = zero
            for slot in downward:
                ref[x, slot, top:top + 8] = zero
        return carry

    lax.fori_loop(0, lx + 2, fill, 0)
    for ref in (f0, f1):
        for x, ex in ((0, 1), (lx + 1, -1)):
            for ey in (1, -1):
                ref[x, SLOT[(ex, ey)], PAD:top] = jnp.zeros((ly, lz), jnp.float32)
    for flag, rows in ((down, slice(0, 8)), (up, slice(top, top + 8))):
        @pl.when(jnp.logical_not(flag))
        def _():
            for ref in (p0, p1):
                for x in range(lx + 2):
                    ref[x, rows] = zero

    load_labels.wait()
    for x in range(lx):
        p0[1 + x, PAD:top] = jnp.where(labels_ref[x] > 0, 1.0, -1.0).astype(jnp.float32)
    pl.semaphore_wait(barrier, 2 + 3 * (up.astype(jnp.int32) + down.astype(jnp.int32)))
    each(pm0, None, "start")

    def solid_at(x, r):
        rows = gy * ly + r + lax.broadcasted_iota(jnp.int32, (tr, lz), 0)
        return (mask_ref[x, pl.ds(r, tr)] > 0) | (rows == 0) | (rows == ny * ly - 1)

    def collide(ref, x, r, f):
        solid = solid_at(x, r)
        relaxed, rho = relax(f)
        rho_ref[x, pl.ds(r, tr)] = rho
        for i in range(19):
            ref[x + 1, SLOT[i], pl.ds(PAD + r, tr)] = jnp.where(solid, f[OPP[i]], relaxed[i])

    def colour(ref, pref, x, r):
        at = pl.ds(PAD + r, tr)
        up_r, dn_r = pl.ds(PAD + 1 + r, tr), pl.ds(PAD - 1 + r, tr)
        p = pref[x + 1, at]
        e, w = pref[x + 2, at], pref[x, at]
        n, s = pref[x + 1, up_r], pref[x + 1, dn_r]
        ne, se = pref[x + 2, up_r], pref[x + 2, dn_r]
        nw, sw = pref[x, up_r], pref[x, dn_r]

        def zsum(v):
            return pltpu.roll(v, 1, 1) + pltpu.roll(v, lz - 1, 1)

        dx, dy = e - w, n - s
        around = (e + w) + (n + s) + 2.0 * p
        ca, cb = ne - sw, se - nw
        twelfth = 1.0 / 12.0
        hx = (2.0 * dx + zsum(dx) + (ca + cb)) * twelfth
        hy = (2.0 * dy + zsum(dy) + (ca - cb)) * twelfth
        hz = (pltpu.roll(around, lz - 1, 1) - pltpu.roll(around, 1, 1)) * twelfth
        xx, yy, zz = hx * hx, hy * hy, hz * hz
        g2 = (xx + yy) + zz
        inv = lax.rsqrt(jnp.maximum(g2, 0.01))
        inv = jnp.where(solid_at(x, r), 0.0, inv)
        rho = rho_ref[x, pl.ds(r, tr)]
        c18 = (0.1 / 18.0) * inv
        c36 = 0.5 * c18
        k18 = (0.175 / 18.0) * (rho * (1.0 - p * p)) * inv
        k36 = 0.5 * k18
        red = 0.5 + 0.5 * p
        total, reds = {}, {}

        def read(i):
            return ref[x + 1, SLOT[i], at]

        def pair(plus, minus, square, k, along):
            shift = k * along
            for i, sign in ((plus, 1), (minus, -1)):
                value = read(i) + square
                total[i] = value
                reds[i] = red * value + shift if sign > 0 else red * value - shift

        total[0] = read(0) + (6.0 * c18) * g2
        reds[0] = red * total[0]
        pair(1, 2, c18 * (xx - g2), k18, hx)
        pair(3, 4, c18 * (yy - g2), k18, hy)
        pair(5, 6, c18 * (zz - g2), k18, hz)
        for plus, minus, along in ((7, 8, hx + hy), (9, 10, hx - hy), (11, 12, hx + hz),
                                   (13, 14, hx - hz), (15, 16, hy + hz), (17, 18, hy - hz)):
            pair(plus, minus, c36 * (along * along - g2), k36, along)
        sums = {}
        for i, (ex, ey, ez) in enumerate(E):
            value, part = total[i], reds[i]
            if ez != 0:
                value = pltpu.roll(value, ez % lz, 1)
                part = pltpu.roll(part, ez % lz, 1)
            ref[x + 1, SLOT[i], at] = value
            sums[(ex, ey)] = sums[(ex, ey)] + part if (ex, ey) in sums else part
        for key, value in sums.items():
            ref[x + 1, SLOT[key], at] = value

    def pull(ref, x, r, key, ex, ey):
        return ref[x + 1 - ex, SLOT[key], pl.ds(PAD - ey + r, tr)]

    def arrive(ref, x, r):
        return [pull(ref, x, r, i, e[0], e[1]) for i, e in enumerate(E)]

    def tree(values):
        while len(values) > 1:
            values = [sum(values[i:i + 2]) for i in range(0, len(values), 2)]
        return values[0]

    def mix(ref, x, r, f):
        red = tree([pull(ref, x, r, key, *key) for key in RED])
        return 2.0 * red / tree(list(f)) - 1.0

    load_mask.wait()

    def first_plane(x, carry):
        load_plane(x).wait()

        def step(t, carry):
            r = pl.multiple_of(t * tr, 8)
            collide(f0, x, r, [pops_ref[i, x, pl.ds(r, tr)] for i in range(19)])
            return carry

        return lax.fori_loop(0, rt, step, carry)

    lax.fori_loop(0, lx, first_plane, 0)
    each(pm0, None, "wait_recv")
    loop("edge", functools.partial(colour, f0, p0))
    gather_red(f0)
    each(fm0, "x", "start")
    loop("inner", functools.partial(colour, f0, p0))
    pack(f0, y0)
    each(fm0, "y", "start")
    each(fm0, "y", "wait_recv")
    unpack(f0, y0)

    def inner(x, r):
        f = arrive(f0, x, r)
        p1[x + 1, pl.ds(PAD + r, tr)] = mix(f0, x, r, f)
        collide(f1, x, r, f)

    loop("inner", inner)
    each(fm0, "x", "wait_recv")

    def edge_phase(x, r):
        p1[x + 1, pl.ds(PAD + r, tr)] = mix(f0, x, r, arrive(f0, x, r))

    loop("edge", edge_phase)
    each(pm1, None, "start")
    loop("edge", lambda x, r: collide(f1, x, r, arrive(f0, x, r)))
    each(pm1, None, "wait_recv")
    loop("edge", functools.partial(colour, f1, p1))
    gather_red(f1)
    each(fm1, "x", "start")
    loop("inner", functools.partial(colour, f1, p1))
    pack(f1, y1)
    each(fm1, "y", "start")
    each(fm1, "y", "wait_recv")
    unpack(f1, y1)

    def store_plane(x):
        return pltpu.make_async_copy(pops_ref.at[:, x], out_hbm.at[:, x], store_sem.at[x])

    def finish(first_x, stride, count):
        def plane(n, carry):
            x = first_x + n * stride

            def step(t, carry):
                r = pl.multiple_of(t * tr, 8)
                f = arrive(f1, x, r)
                for i in range(19):
                    pops_ref[i, x, pl.ds(r, tr)] = f[i]
                rho_ref[x, pl.ds(r, tr)] = mix(f1, x, r, f)
                return carry

            lax.fori_loop(0, rt, step, 0)
            store_plane(x).start()
            return carry

        lax.fori_loop(0, count, plane, 0)

    finish(1, 1, lx - 2)
    each(fm1, "x", "wait_recv")
    finish(0, lx - 1, 2)
    store_phase = pltpu.make_async_copy(rho_ref, phase_hbm, store_sem.at[lx])
    store_phase.start()
    for messages in (pm0, fm0, pm1, fm1):
        each(messages, None, "wait_send")
    for x in range(lx):
        store_plane(x).wait()
    store_phase.wait()


def solution(mesh):
    nx, ny = mesh.shape["gx"], mesh.shape["gy"]

    def on_device(populations, labels, solid_mask):
        lx, ly, lz = labels.shape
        rows = ly + 2 * PAD
        return pl.pallas_call(
            functools.partial(kernel, nx, ny),
            out_shape=(jax.ShapeDtypeStruct((19, lx, ly, lz), jnp.float32),
                       jax.ShapeDtypeStruct((lx, ly, lz), jnp.float32)),
            in_specs=[pl.BlockSpec(memory_space=pltpu.HBM)] * 3,
            out_specs=(pl.BlockSpec(memory_space=pltpu.HBM),) * 2,
            scratch_shapes=[
                pltpu.VMEM((lx + 2, NS, rows, lz), jnp.float32),
                pltpu.VMEM((lx + 2, NS, rows, lz), jnp.float32),
                pltpu.VMEM((lx + 2, rows, lz), jnp.float32),
                pltpu.VMEM((lx + 2, rows, lz), jnp.float32),
                pltpu.VMEM((lx, ly, lz), jnp.float32),
                pltpu.VMEM((19, lx, ly, lz), jnp.float32),
                pltpu.VMEM((lx, ly, lz), jnp.int32),
                pltpu.VMEM((lx, ly, lz), jnp.int32),
                pltpu.VMEM((4, lx, 8, lz), jnp.float32),
                pltpu.VMEM((4, lx, 8, lz), jnp.float32),
                pltpu.SemaphoreType.DMA((lx + 2,)),
                pltpu.SemaphoreType.DMA((lx + 1,)),
                pltpu.SemaphoreType.DMA((32,)),
                pltpu.SemaphoreType.DMA((32,)),
            ],
            compiler_params=pltpu.CompilerParams(
                collective_id=0, has_side_effects=True, vmem_limit_bytes=64 * 2**20),
        )(populations, labels, solid_mask)

    return jax.shard_map(
        on_device, mesh=mesh,
        in_specs=(P(None, "gx", "gy", None), P("gx", "gy", None), P("gx", "gy", None)),
        out_specs=(P(None, "gx", "gy", None), P("gx", "gy", None)),
        check_vma=False)
```

```python
import functools

import jax
import jax.numpy as jnp
from jax import lax
from jax.experimental import pallas as pl
from jax.experimental.pallas import tpu as pltpu
from jax.sharding import PartitionSpec as P

E = [
    (0, 0, 0), (1, 0, 0), (-1, 0, 0), (0, 1, 0), (0, -1, 0), (0, 0, 1), (0, 0, -1),
    (1, 1, 0), (-1, -1, 0), (1, -1, 0), (-1, 1, 0), (1, 0, 1), (-1, 0, -1), (1, 0, -1),
    (-1, 0, 1), (0, 1, 1), (0, -1, -1), (0, 1, -1), (0, -1, 1),
]
OPP = [0, 2, 1, 4, 3, 6, 5, 8, 7, 10, 9, 12, 11, 14, 13, 16, 15, 18, 17]
ORDER = [
    (1, -1), 9, 1, 11, 13, (1, 0), 7, (1, 1),
    3, 15, 17, (0, 1), (-1, 1), 10,
    2, 12, 14, (-1, 0), 8, (-1, -1),
    4, 16, 18, (0, -1),
    0, 5, 6, (0, 0),
]
SLOT = {key: place for place, key in enumerate(ORDER)}
RED = [key for key in ORDER if isinstance(key, tuple)]
NS = len(ORDER)
PAD = 8
MESH = pl.DeviceIdType.MESH


def relax(f):
    def plane(pp, mm, pm, mp):
        s1, d1, s2, d2 = f[pp] + f[mm], f[pp] - f[mm], f[pm] + f[mp], f[pm] - f[mp]
        return s1 + s2, s1 - s2, d1 + d2, d1 - d2

    xy = plane(7, 8, 9, 10)
    xz = plane(11, 12, 13, 14)
    yz = plane(15, 16, 17, 18)
    sx, sy, sz = f[1] + f[2], f[3] + f[4], f[5] + f[6]
    rho = (f[0] + sx) + (sy + sz) + ((xy[0] + xz[0]) + yz[0])
    jx = (f[1] - f[2]) + (xy[2] + xz[2])
    jy = (f[3] - f[4]) + (xy[3] + yz[2])
    jz = (f[5] - f[6]) + (xz[3] + yz[3])
    inv = 1.0 / rho
    ux, uy, uz = jx * inv, jy * inv, jz * inv
    qx, qy, qz = jx * ux, jy * uy, jz * uz
    third = rho * (1.0 / 3.0)
    dxx = (sx + (xy[0] + xz[0])) - (third + qx)
    dyy = (sy + (xy[0] + yz[0])) - (third + qy)
    dzz = (sz + (xz[0] + yz[0])) - (third + qz)
    trace = (dxx + dyy) + dzz
    part = trace * (1.0 / 12.0)
    base = rho * (1.0 / 9.0) + ((qx + qy) + qz) * (1.0 / 3.0)
    tx, ty, tz = jx * (1.0 / 3.0), jy * (1.0 / 3.0), jz * (1.0 / 3.0)
    out = list(f)

    def edges(moments, rest, cross, ta, tb, pp, mm, pm, mp):
        four = (moments[0] - base) + 0.5 * rest
        a = 0.35 * four
        d = 0.3125 * (moments[1] - cross)
        b = 0.3 * (moments[2] - ta)
        c = 0.3 * (moments[3] - tb)
        p1, p2, q1, q2 = a + d, a - d, b + c, b - c
        out[pp] = f[pp] - (p1 + q1)
        out[mm] = f[mm] - (p1 - q1)
        out[pm] = f[pm] - (p2 + q2)
        out[mp] = f[mp] - (p2 - q2)
        return a, b, c

    axy, bxy, cxy = edges(xy, qz, jx * uy, tx, ty, 7, 8, 9, 10)
    axz, bxz, cxz = edges(xz, qy, jx * uz, tx, tz, 11, 12, 13, 14)
    ayz, byz, cyz = edges(yz, qx, jy * uz, ty, tz, 15, 16, 17, 18)

    def faces(delta, a, b, plus, minus):
        half = (0.625 * delta - 0.5 * part) - 2.0 * a
        diff = 2.0 * b
        out[plus] = f[plus] - (half - diff)
        out[minus] = f[minus] - (half + diff)

    faces(dxx, axy + axz, bxy + bxz, 1, 2)
    faces(dyy, axy + ayz, cxy + byz, 3, 4)
    faces(dzz, axz + ayz, cxz + cyz, 5, 6)
    out[0] = f[0] + (trace - 4.0 * ((axy + axz) + ayz))
    return out, rho


def kernel(nx, ny, pops_hbm, code_ref, out_ref, phase_ref,
           f0, f1, p0, p1, rho_ref, pops_ref, y0, y1, load_sem,
           send_sem, recv_sem):
    lx, ly, lz = code_ref.shape
    tr = 32 if ly % 32 == 0 else 8
    rt = ly // tr
    top = PAD + ly
    gx, gy = lax.axis_index("gx"), lax.axis_index("gy")
    xp, xm = lax.rem(gx + 1, nx), lax.rem(gx + nx - 1, nx)
    up, down = gy < ny - 1, gy > 0

    barrier = pltpu.get_barrier_semaphore()

    def greet(ax, ay):
        pl.semaphore_signal(barrier, inc=1, device_id=(ax, ay), device_id_type=MESH)

    greet(xp, gy)
    greet(xm, gy)
    for flag, ay in ((up, gy + 1), (down, gy - 1)):
        @pl.when(flag)
        def _():
            greet(gx, ay)
            greet(xp, ay)
            greet(xm, ay)

    def load_plane(x):
        return pltpu.make_async_copy(pops_hbm.at[:, x], pops_ref.at[:, x], load_sem.at[x])

    for x in range(lx):
        load_plane(x).start()

    def move(ref, src, dst, k, ax, ay):
        return pltpu.make_async_remote_copy(
            src_ref=ref.at[src], dst_ref=ref.at[dst],
            send_sem=send_sem.at[k], recv_sem=recv_sem.at[k],
            device_id=(ax, ay), device_id_type=MESH)

    mid = pl.ds(PAD, ly)
    last, ghost_low = pl.ds(top - 8, 8), pl.ds(0, 8)
    first, ghost_high = pl.ds(PAD, 8), pl.ds(top, 8)
    own = pl.ds(1, lx)

    def phase_messages(ref, k):
        return [
            ("x", move(ref, (lx, mid), (0, mid), k, xp, gy), None, None),
            ("x", move(ref, (1, mid), (lx + 1, mid), k + 1, xm, gy), None, None),
            ("y", move(ref, (own, last), (own, ghost_low), k + 2, gx, gy + 1), up, down),
            ("y", move(ref, (own, first), (own, ghost_high), k + 3, gx, gy - 1), down, up),
            ("x", move(ref, (lx, last), (0, ghost_low), k + 4, xp, gy + 1), up, down),
            ("x", move(ref, (1, last), (lx + 1, ghost_low), k + 5, xm, gy + 1), up, down),
            ("x", move(ref, (lx, first), (0, ghost_high), k + 6, xp, gy - 1), down, up),
            ("x", move(ref, (1, first), (lx + 1, ghost_high), k + 7, xm, gy - 1), down, up),
        ]

    def field_messages(ref, rows, k):
        def s(a, b):
            return pl.ds(a, b - a)

        return [
            ("x+", move(ref, (lx, s(1, 7), mid), (0, s(1, 7), mid), k, xp, gy), None, None),
            ("x-", move(ref, (1, s(13, 19), mid), (lx + 1, s(13, 19), mid), k + 1, xm, gy),
             None, None),
            ("x+", move(ref, (lx, s(6, 8), last), (0, s(6, 8), ghost_low), k + 2, xp, gy + 1),
             up, down),
            ("x-", move(ref, (1, s(12, 14), last), (lx + 1, s(12, 14), ghost_low), k + 3, xm,
                       gy + 1), up, down),
            ("x+", move(ref, (lx, s(0, 2), first), (0, s(0, 2), ghost_high), k + 4, xp, gy - 1),
             down, up),
            ("x-", move(ref, (1, s(18, 20), first), (lx + 1, s(18, 20), ghost_high), k + 5, xm,
                       gy - 1), down, up),
            ("y", move(rows, 0, 1, k + 6, gx, gy + 1), up, down),
            ("y", move(rows, 2, 3, k + 7, gx, gy - 1), down, up),
        ]

    upward = list(range(6, 14))
    downward = list(range(18, 24)) + [0, 1]

    def pack(ref, rows):
        for flag, slots, place, row in ((up, upward, 0, top - 1), (down, downward, 2, PAD)):
            @pl.when(flag)
            def _():
                for x in range(lx):
                    for k, slot in enumerate(slots):
                        rows[place, x, k:k + 1] = ref[x + 1, slot, row:row + 1]

    def unpack(ref, rows):
        for flag, slots, place, row in ((down, upward, 1, PAD - 1), (up, downward, 3, top)):
            @pl.when(flag)
            def _():
                for x in range(lx):
                    for k, slot in enumerate(slots):
                        ref[x + 1, slot, row:row + 1] = rows[place, x, k:k + 1]

    def gather_red(ref, x, ex):
        ref[x, SLOT[(ex, 0)], PAD:top] = (
            ref[x, SLOT[(ex, 0)], PAD:top] + ref[x, SLOT[(ex, 1)], PAD - 1:top - 1]
            + ref[x, SLOT[(ex, -1)], PAD + 1:top + 1])

    def each(messages, kind, action):
        for name, copy, sends, receives in messages:
            if kind is not None and kind not in name:
                continue
            flag = receives if action == "wait_recv" else sends
            if flag is None:
                getattr(copy, action)()
            else:
                pl.when(flag)(getattr(copy, action))

    pm0, fm0 = phase_messages(p0, 0), field_messages(f0, y0, 8)
    pm1, fm1 = phase_messages(p1, 16), field_messages(f1, y1, 24)

    def loop(kind, body):
        count = {"edge": 2, "inner": lx - 2, "low": 1, "high": 1}[kind]

        def step(t, carry):
            plane, row = t // rt, lax.rem(t, rt)
            if kind == "edge":
                plane = plane * (lx - 1)
            elif kind == "high":
                plane = plane + (lx - 1)
            elif kind == "inner":
                plane = plane + 1
            body(plane, pl.multiple_of(row * tr, 8))
            return carry

        lax.fori_loop(0, count * rt, step, 0)

    zero = jnp.zeros((8, lz), jnp.float32)

    def fill(x, carry):
        for ref in (f0, f1):
            for slot in upward:
                ref[x, slot, 0:8] = zero
            for slot in downward:
                ref[x, slot, top:top + 8] = zero
        return carry

    lax.fori_loop(0, lx + 2, fill, 0)
    for ref in (f0, f1):
        for x, ex in ((0, 1), (lx + 1, -1)):
            for ey in (1, -1):
                ref[x, SLOT[(ex, ey)], PAD:top] = jnp.zeros((ly, lz), jnp.float32)
    for flag, rows in ((down, slice(0, 8)), (up, slice(top, top + 8))):
        @pl.when(jnp.logical_not(flag))
        def _():
            for ref in (p0, p1):
                for x in range(lx + 2):
                    ref[x, rows] = zero

    for x in range(lx):
        p0[1 + x, PAD:top] = jnp.where((code_ref[x] & 1) > 0, 1.0, -1.0).astype(jnp.float32)
    pl.semaphore_wait(barrier, 2 + 3 * (up.astype(jnp.int32) + down.astype(jnp.int32)))
    each(pm0, None, "start")

    def solid_at(x, r):
        return code_ref[x, pl.ds(r, tr)] > 1

    def collide(ref, x, r, f):
        solid = solid_at(x, r)
        relaxed, rho = relax(f)
        rho_ref[x, pl.ds(r, tr)] = rho
        for i in range(19):
            ref[x + 1, SLOT[i], pl.ds(PAD + r, tr)] = jnp.where(solid, f[OPP[i]], relaxed[i])

    def colour(ref, pref, x, r):
        at = pl.ds(PAD + r, tr)
        up_r, dn_r = pl.ds(PAD + 1 + r, tr), pl.ds(PAD - 1 + r, tr)
        p = pref[x + 1, at]
        e, w = pref[x + 2, at], pref[x, at]
        n, s = pref[x + 1, up_r], pref[x + 1, dn_r]
        ne, se = pref[x + 2, up_r], pref[x + 2, dn_r]
        nw, sw = pref[x, up_r], pref[x, dn_r]

        def zsum(v):
            return pltpu.roll(v, 1, 1) + pltpu.roll(v, lz - 1, 1)

        dx, dy = e - w, n - s
        around = (e + w) + (n + s) + 2.0 * p
        ca, cb = ne - sw, se - nw
        twelfth = 1.0 / 12.0
        hx = (2.0 * dx + zsum(dx) + (ca + cb)) * twelfth
        hy = (2.0 * dy + zsum(dy) + (ca - cb)) * twelfth
        hz = (pltpu.roll(around, lz - 1, 1) - pltpu.roll(around, 1, 1)) * twelfth
        xx, yy, zz = hx * hx, hy * hy, hz * hz
        g2 = (xx + yy) + zz
        inv = lax.rsqrt(jnp.maximum(g2, 0.01))
        inv = jnp.where(solid_at(x, r), 0.0, inv)
        rho = rho_ref[x, pl.ds(r, tr)]
        c18 = (0.1 / 18.0) * inv
        c36 = 0.5 * c18
        k18 = (0.175 / 18.0) * (rho * (1.0 - p * p)) * inv
        k36 = 0.5 * k18
        red = 0.5 + 0.5 * p
        total, reds = {}, {}

        def read(i):
            return ref[x + 1, SLOT[i], at]

        def pair(plus, minus, square, k, along):
            shift = k * along
            for i, sign in ((plus, 1), (minus, -1)):
                value = read(i) + square
                total[i] = value
                reds[i] = red * value + shift if sign > 0 else red * value - shift

        total[0] = read(0) + (6.0 * c18) * g2
        reds[0] = red * total[0]
        pair(1, 2, c18 * (xx - g2), k18, hx)
        pair(3, 4, c18 * (yy - g2), k18, hy)
        pair(5, 6, c18 * (zz - g2), k18, hz)
        for plus, minus, along in ((7, 8, hx + hy), (9, 10, hx - hy), (11, 12, hx + hz),
                                   (13, 14, hx - hz), (15, 16, hy + hz), (17, 18, hy - hz)):
            pair(plus, minus, c36 * (along * along - g2), k36, along)
        sums = {}
        for i, (ex, ey, ez) in enumerate(E):
            value, part = total[i], reds[i]
            if ez != 0:
                value = pltpu.roll(value, ez % lz, 1)
                part = pltpu.roll(part, ez % lz, 1)
            ref[x + 1, SLOT[i], at] = value
            sums[(ex, ey)] = sums[(ex, ey)] + part if (ex, ey) in sums else part
        for key, value in sums.items():
            ref[x + 1, SLOT[key], at] = value

    def pull(ref, x, r, key, ex, ey):
        return ref[x + 1 - ex, SLOT[key], pl.ds(PAD - ey + r, tr)]

    def arrive(ref, x, r):
        return [pull(ref, x, r, i, e[0], e[1]) for i, e in enumerate(E)]

    def tree(values):
        while len(values) > 1:
            values = [sum(values[i:i + 2]) for i in range(0, len(values), 2)]
        return values[0]

    def mix(ref, x, r, f):
        red = tree([pull(ref, x, r, key, *key) for key in RED])
        return 2.0 * red / tree(list(f)) - 1.0


    def first_plane(x, carry):
        load_plane(x).wait()

        def step(t, carry):
            r = pl.multiple_of(t * tr, 8)
            collide(f0, x, r, [pops_ref[i, x, pl.ds(r, tr)] for i in range(19)])
            return carry

        return lax.fori_loop(0, rt, step, carry)

    lax.fori_loop(0, lx, first_plane, 0)
    each(pm0, None, "wait_recv")
    for side, x, ex, name in (("high", lx, 1, "x+"), ("low", 1, -1, "x-")):
        loop(side, functools.partial(colour, f0, p0))
        gather_red(f0, x, ex)
        each(fm0, name, "start")
    loop("inner", functools.partial(colour, f0, p0))
    pack(f0, y0)
    each(fm0, "y", "start")
    each(fm0, "y", "wait_recv")
    unpack(f0, y0)

    def inner(x, r):
        f = arrive(f0, x, r)
        p1[x + 1, pl.ds(PAD + r, tr)] = mix(f0, x, r, f)
        collide(f1, x, r, f)

    loop("inner", inner)
    each(fm0, "x", "wait_recv")

    def edge_phase(x, r):
        p1[x + 1, pl.ds(PAD + r, tr)] = mix(f0, x, r, arrive(f0, x, r))

    loop("edge", edge_phase)
    each(pm1, None, "start")
    loop("edge", lambda x, r: collide(f1, x, r, arrive(f0, x, r)))
    each(pm1, None, "wait_recv")
    for side, x, ex, name in (("high", lx, 1, "x+"), ("low", 1, -1, "x-")):
        loop(side, functools.partial(colour, f1, p1))
        gather_red(f1, x, ex)
        each(fm1, name, "start")
    loop("inner", functools.partial(colour, f1, p1))
    pack(f1, y1)
    each(fm1, "y", "start")
    each(fm1, "y", "wait_recv")
    unpack(f1, y1)

    def finish(first_x, stride, count):
        def plane(n, carry):
            x = first_x + n * stride

            def step(t, carry):
                r = pl.multiple_of(t * tr, 8)
                f = arrive(f1, x, r)
                for i in range(19):
                    out_ref[i, x, pl.ds(r, tr)] = f[i]
                phase_ref[x, pl.ds(r, tr)] = mix(f1, x, r, f)
                return carry

            return lax.fori_loop(0, rt, step, carry)

        lax.fori_loop(0, count, plane, 0)

    finish(1, 1, lx - 2)
    each(fm1, "x", "wait_recv")
    finish(0, lx - 1, 2)
    for messages in (pm0, fm0, pm1, fm1):
        each(messages, None, "wait_send")


def solution(mesh):
    nx, ny = mesh.shape["gx"], mesh.shape["gy"]

    def on_device(populations, labels, solid_mask):
        lx, ly, lz = labels.shape
        rows = ly + 2 * PAD
        y = lax.axis_index("gy") * ly + lax.broadcasted_iota(jnp.int32, (lx, ly, lz), 1)
        solid = (solid_mask > 0) | (y == 0) | (y == ny * ly - 1)
        code = jnp.where(labels > 0, 1, 0) + jnp.where(solid, 2, 0)
        return pl.pallas_call(
            functools.partial(kernel, nx, ny),
            out_shape=(jax.ShapeDtypeStruct((19, lx, ly, lz), jnp.float32),
                       jax.ShapeDtypeStruct((lx, ly, lz), jnp.float32)),
            in_specs=[pl.BlockSpec(memory_space=pltpu.HBM), pl.BlockSpec(memory_space=pltpu.VMEM)],
            out_specs=(pl.BlockSpec(memory_space=pltpu.VMEM),) * 2,
            scratch_shapes=[
                pltpu.VMEM((lx + 2, NS, rows, lz), jnp.float32),
                pltpu.VMEM((lx + 2, NS, rows, lz), jnp.float32),
                pltpu.VMEM((lx + 2, rows, lz), jnp.float32),
                pltpu.VMEM((lx + 2, rows, lz), jnp.float32),
                pltpu.VMEM((lx, ly, lz), jnp.float32),
                pltpu.VMEM((19, lx, ly, lz), jnp.float32),
                pltpu.VMEM((4, lx, 8, lz), jnp.float32),
                pltpu.VMEM((4, lx, 8, lz), jnp.float32),
                pltpu.SemaphoreType.DMA((lx,)),
                pltpu.SemaphoreType.DMA((32,)),
                pltpu.SemaphoreType.DMA((32,)),
            ],
            compiler_params=pltpu.CompilerParams(
                collective_id=0, has_side_effects=True, vmem_limit_bytes=52 * 2**20),
        )(populations, code)

    return jax.shard_map(
        on_device, mesh=mesh,
        in_specs=(P(None, "gx", "gy", None), P("gx", "gy", None), P("gx", "gy", None)),
        out_specs=(P(None, "gx", "gy", None), P("gx", "gy", None)),
        check_vma=False)
```

```python
import functools

import jax
import jax.numpy as jnp
from jax import lax
from jax.experimental import pallas as pl
from jax.experimental.pallas import tpu as pltpu
from jax.sharding import PartitionSpec as P

E = [
    (0, 0, 0), (1, 0, 0), (-1, 0, 0), (0, 1, 0), (0, -1, 0), (0, 0, 1), (0, 0, -1),
    (1, 1, 0), (-1, -1, 0), (1, -1, 0), (-1, 1, 0), (1, 0, 1), (-1, 0, -1), (1, 0, -1),
    (-1, 0, 1), (0, 1, 1), (0, -1, -1), (0, 1, -1), (0, -1, 1),
]
OPP = [0, 2, 1, 4, 3, 6, 5, 8, 7, 10, 9, 12, 11, 14, 13, 16, 15, 18, 17]
ORDER = [
    (1, -1), 9, 1, 11, 13, (1, 0), 7, (1, 1),
    3, 15, 17, (0, 1), (-1, 1), 10,
    2, 12, 14, (-1, 0), 8, (-1, -1),
    4, 16, 18, (0, -1),
    0, 5, 6, (0, 0),
]
SLOT = {key: place for place, key in enumerate(ORDER)}
RED = [key for key in ORDER if isinstance(key, tuple)]
NS = len(ORDER)
PAD = 8
MESH = pl.DeviceIdType.MESH


def relax(f):
    def plane(pp, mm, pm, mp):
        s1, d1, s2, d2 = f[pp] + f[mm], f[pp] - f[mm], f[pm] + f[mp], f[pm] - f[mp]
        return s1 + s2, s1 - s2, d1 + d2, d1 - d2

    xy = plane(7, 8, 9, 10)
    xz = plane(11, 12, 13, 14)
    yz = plane(15, 16, 17, 18)
    sx, sy, sz = f[1] + f[2], f[3] + f[4], f[5] + f[6]
    rho = (f[0] + sx) + (sy + sz) + ((xy[0] + xz[0]) + yz[0])
    jx = (f[1] - f[2]) + (xy[2] + xz[2])
    jy = (f[3] - f[4]) + (xy[3] + yz[2])
    jz = (f[5] - f[6]) + (xz[3] + yz[3])
    inv = 1.0 / rho
    ux, uy, uz = jx * inv, jy * inv, jz * inv
    qx, qy, qz = jx * ux, jy * uy, jz * uz
    third = rho * (1.0 / 3.0)
    dxx = (sx + (xy[0] + xz[0])) - (third + qx)
    dyy = (sy + (xy[0] + yz[0])) - (third + qy)
    dzz = (sz + (xz[0] + yz[0])) - (third + qz)
    trace = (dxx + dyy) + dzz
    part = trace * (1.0 / 12.0)
    base = rho * (1.0 / 9.0) + ((qx + qy) + qz) * (1.0 / 3.0)
    tx, ty, tz = jx * (1.0 / 3.0), jy * (1.0 / 3.0), jz * (1.0 / 3.0)
    out = list(f)

    def edges(moments, rest, cross, ta, tb, pp, mm, pm, mp):
        four = (moments[0] - base) + 0.5 * rest
        a = 0.35 * four
        d = 0.3125 * (moments[1] - cross)
        b = 0.3 * (moments[2] - ta)
        c = 0.3 * (moments[3] - tb)
        p1, p2, q1, q2 = a + d, a - d, b + c, b - c
        out[pp] = f[pp] - (p1 + q1)
        out[mm] = f[mm] - (p1 - q1)
        out[pm] = f[pm] - (p2 + q2)
        out[mp] = f[mp] - (p2 - q2)
        return a, b, c

    axy, bxy, cxy = edges(xy, qz, jx * uy, tx, ty, 7, 8, 9, 10)
    axz, bxz, cxz = edges(xz, qy, jx * uz, tx, tz, 11, 12, 13, 14)
    ayz, byz, cyz = edges(yz, qx, jy * uz, ty, tz, 15, 16, 17, 18)

    def faces(delta, a, b, plus, minus):
        half = (0.625 * delta - 0.5 * part) - 2.0 * a
        diff = 2.0 * b
        out[plus] = f[plus] - (half - diff)
        out[minus] = f[minus] - (half + diff)

    faces(dxx, axy + axz, bxy + bxz, 1, 2)
    faces(dyy, axy + ayz, cxy + byz, 3, 4)
    faces(dzz, axz + ayz, cxz + cyz, 5, 6)
    out[0] = f[0] + (trace - 4.0 * ((axy + axz) + ayz))
    return out, rho


def kernel(nx, ny, pops_hbm, code_ref, out_ref, phase_ref,
           f0, f1, p0, p1, rho_ref, pops_ref, y0, y1, load_sem,
           send_sem, recv_sem):
    lx, ly, lz = code_ref.shape
    tr = 32 if ly % 32 == 0 else 8
    rt = ly // tr
    top = PAD + ly
    gx, gy = lax.axis_index("gx"), lax.axis_index("gy")
    xp, xm = lax.rem(gx + 1, nx), lax.rem(gx + nx - 1, nx)
    up, down = gy < ny - 1, gy > 0

    barrier = pltpu.get_barrier_semaphore()

    def greet(ax, ay):
        pl.semaphore_signal(barrier, inc=1, device_id=(ax, ay), device_id_type=MESH)

    greet(xp, gy)
    greet(xm, gy)
    for flag, ay in ((up, gy + 1), (down, gy - 1)):
        @pl.when(flag)
        def _():
            greet(gx, ay)
            greet(xp, ay)
            greet(xm, ay)

    def load_plane(x):
        return pltpu.make_async_copy(pops_hbm.at[:, x], pops_ref.at[:, x], load_sem.at[x])

    for x in range(lx):
        load_plane(x).start()

    def move(ref, src, dst, k, ax, ay):
        return pltpu.make_async_remote_copy(
            src_ref=ref.at[src], dst_ref=ref.at[dst],
            send_sem=send_sem.at[k], recv_sem=recv_sem.at[k],
            device_id=(ax, ay), device_id_type=MESH)

    mid = pl.ds(PAD, ly)
    last, ghost_low = pl.ds(top - 8, 8), pl.ds(0, 8)
    first, ghost_high = pl.ds(PAD, 8), pl.ds(top, 8)
    own = pl.ds(1, lx)

    def phase_messages(ref, k):
        return [
            ("x+", move(ref, (lx, mid), (0, mid), k, xp, gy), None, None),
            ("x-", move(ref, (1, mid), (lx + 1, mid), k + 1, xm, gy), None, None),
            ("y", move(ref, (own, last), (own, ghost_low), k + 2, gx, gy + 1), up, down),
            ("y", move(ref, (own, first), (own, ghost_high), k + 3, gx, gy - 1), down, up),
            ("x+", move(ref, (lx, last), (0, ghost_low), k + 4, xp, gy + 1), up, down),
            ("x-", move(ref, (1, last), (lx + 1, ghost_low), k + 5, xm, gy + 1), up, down),
            ("x+", move(ref, (lx, first), (0, ghost_high), k + 6, xp, gy - 1), down, up),
            ("x-", move(ref, (1, first), (lx + 1, ghost_high), k + 7, xm, gy - 1), down, up),
        ]

    def field_messages(ref, rows, k):
        def s(a, b):
            return pl.ds(a, b - a)

        return [
            ("x+", move(ref, (lx, s(1, 7), mid), (0, s(1, 7), mid), k, xp, gy), None, None),
            ("x-", move(ref, (1, s(13, 19), mid), (lx + 1, s(13, 19), mid), k + 1, xm, gy),
             None, None),
            ("x+", move(ref, (lx, s(6, 8), last), (0, s(6, 8), ghost_low), k + 2, xp, gy + 1),
             up, down),
            ("x-", move(ref, (1, s(12, 14), last), (lx + 1, s(12, 14), ghost_low), k + 3, xm,
                       gy + 1), up, down),
            ("x+", move(ref, (lx, s(0, 2), first), (0, s(0, 2), ghost_high), k + 4, xp, gy - 1),
             down, up),
            ("x-", move(ref, (1, s(18, 20), first), (lx + 1, s(18, 20), ghost_high), k + 5, xm,
                       gy - 1), down, up),
            ("y", move(rows, 0, 1, k + 6, gx, gy + 1), up, down),
            ("y", move(rows, 2, 3, k + 7, gx, gy - 1), down, up),
        ]

    upward = list(range(6, 14))
    downward = list(range(18, 24)) + [0, 1]

    def pack(ref, rows):
        for flag, slots, place, row in ((up, upward, 0, top - 1), (down, downward, 2, PAD)):
            @pl.when(flag)
            def _():
                for x in range(lx):
                    for k, slot in enumerate(slots):
                        rows[place, x, k:k + 1] = ref[x + 1, slot, row:row + 1]

    def unpack(ref, rows):
        for flag, slots, place, row in ((down, upward, 1, PAD - 1), (up, downward, 3, top)):
            @pl.when(flag)
            def _():
                for x in range(lx):
                    for k, slot in enumerate(slots):
                        ref[x + 1, slot, row:row + 1] = rows[place, x, k:k + 1]

    def gather_red(ref, x, ex):
        ref[x, SLOT[(ex, 0)], PAD:top] = (
            ref[x, SLOT[(ex, 0)], PAD:top] + ref[x, SLOT[(ex, 1)], PAD - 1:top - 1]
            + ref[x, SLOT[(ex, -1)], PAD + 1:top + 1])

    def each(messages, kind, action):
        for name, copy, sends, receives in messages:
            if kind is not None and kind not in name:
                continue
            flag = receives if action == "wait_recv" else sends
            if flag is None:
                getattr(copy, action)()
            else:
                pl.when(flag)(getattr(copy, action))

    pm0, fm0 = phase_messages(p0, 0), field_messages(f0, y0, 8)
    pm1, fm1 = phase_messages(p1, 16), field_messages(f1, y1, 24)

    odd = lax.rem(gx, 2)

    def sides(near_first, body, before=None, after=None):
        def side(n, carry):
            pick = lax.rem(n + odd + (1 if near_first else 0), 2)
            for action in (before, body, after):
                if action is body:
                    plane = pick * (lx - 1)
                    lax.fori_loop(
                        0, rt, lambda t, c: body(plane, pl.multiple_of(t * tr, 8)) or c, 0)
                elif action is not None:
                    pl.when(pick == 0)(lambda: action(True))
                    pl.when(pick == 1)(lambda: action(False))
            return carry

        lax.fori_loop(0, 2, side, 0)

    def loop(kind, body):
        count = {"edge": 2, "inner": lx - 2}[kind]

        def step(t, carry):
            plane, row = t // rt, lax.rem(t, rt)
            if kind == "edge":
                plane = plane * (lx - 1)
            elif kind == "inner":
                plane = plane + 1
            body(plane, pl.multiple_of(row * tr, 8))
            return carry

        lax.fori_loop(0, count * rt, step, 0)

    zero = jnp.zeros((8, lz), jnp.float32)

    def fill(x, carry):
        for ref in (f0, f1):
            for slot in upward:
                ref[x, slot, 0:8] = zero
            for slot in downward:
                ref[x, slot, top:top + 8] = zero
        return carry

    lax.fori_loop(0, lx + 2, fill, 0)
    for ref in (f0, f1):
        for x, ex in ((0, 1), (lx + 1, -1)):
            for ey in (1, -1):
                ref[x, SLOT[(ex, ey)], PAD:top] = jnp.zeros((ly, lz), jnp.float32)
    for flag, rows in ((down, slice(0, 8)), (up, slice(top, top + 8))):
        @pl.when(jnp.logical_not(flag))
        def _():
            for ref in (p0, p1):
                for x in range(lx + 2):
                    ref[x, rows] = zero

    for x in range(lx):
        p0[1 + x, PAD:top] = jnp.where((code_ref[x] & 1) > 0, 1.0, -1.0).astype(jnp.float32)
    pl.semaphore_wait(barrier, 2 + 3 * (up.astype(jnp.int32) + down.astype(jnp.int32)))
    each(pm0, None, "start")

    def solid_at(x, r):
        return code_ref[x, pl.ds(r, tr)] > 1

    def collide(ref, x, r, f):
        solid = solid_at(x, r)
        relaxed, rho = relax(f)
        rho_ref[x, pl.ds(r, tr)] = rho
        for i in range(19):
            ref[x + 1, SLOT[i], pl.ds(PAD + r, tr)] = jnp.where(solid, f[OPP[i]], relaxed[i])

    def colour(ref, pref, x, r):
        at = pl.ds(PAD + r, tr)
        up_r, dn_r = pl.ds(PAD + 1 + r, tr), pl.ds(PAD - 1 + r, tr)
        p = pref[x + 1, at]
        e, w = pref[x + 2, at], pref[x, at]
        n, s = pref[x + 1, up_r], pref[x + 1, dn_r]
        ne, se = pref[x + 2, up_r], pref[x + 2, dn_r]
        nw, sw = pref[x, up_r], pref[x, dn_r]

        def zsum(v):
            return pltpu.roll(v, 1, 1) + pltpu.roll(v, lz - 1, 1)

        dx, dy = e - w, n - s
        around = (e + w) + (n + s) + 2.0 * p
        ca, cb = ne - sw, se - nw
        twelfth = 1.0 / 12.0
        hx = (2.0 * dx + zsum(dx) + (ca + cb)) * twelfth
        hy = (2.0 * dy + zsum(dy) + (ca - cb)) * twelfth
        hz = (pltpu.roll(around, lz - 1, 1) - pltpu.roll(around, 1, 1)) * twelfth
        xx, yy, zz = hx * hx, hy * hy, hz * hz
        g2 = (xx + yy) + zz
        inv = lax.rsqrt(jnp.maximum(g2, 0.01))
        inv = jnp.where(solid_at(x, r), 0.0, inv)
        rho = rho_ref[x, pl.ds(r, tr)]
        c18 = (0.1 / 18.0) * inv
        c36 = 0.5 * c18
        k18 = (0.175 / 18.0) * (rho * (1.0 - p * p)) * inv
        k36 = 0.5 * k18
        red = 0.5 + 0.5 * p
        total, reds = {}, {}

        def read(i):
            return ref[x + 1, SLOT[i], at]

        def pair(plus, minus, square, k, along):
            shift = k * along
            for i, sign in ((plus, 1), (minus, -1)):
                value = read(i) + square
                total[i] = value
                reds[i] = red * value + shift if sign > 0 else red * value - shift

        total[0] = read(0) + (6.0 * c18) * g2
        reds[0] = red * total[0]
        pair(1, 2, c18 * (xx - g2), k18, hx)
        pair(3, 4, c18 * (yy - g2), k18, hy)
        pair(5, 6, c18 * (zz - g2), k18, hz)
        for plus, minus, along in ((7, 8, hx + hy), (9, 10, hx - hy), (11, 12, hx + hz),
                                   (13, 14, hx - hz), (15, 16, hy + hz), (17, 18, hy - hz)):
            pair(plus, minus, c36 * (along * along - g2), k36, along)
        sums = {}
        for i, (ex, ey, ez) in enumerate(E):
            value, part = total[i], reds[i]
            if ez != 0:
                value = pltpu.roll(value, ez % lz, 1)
                part = pltpu.roll(part, ez % lz, 1)
            ref[x + 1, SLOT[i], at] = value
            sums[(ex, ey)] = sums[(ex, ey)] + part if (ex, ey) in sums else part
        for key, value in sums.items():
            ref[x + 1, SLOT[key], at] = value

    def pull(ref, x, r, key, ex, ey):
        return ref[x + 1 - ex, SLOT[key], pl.ds(PAD - ey + r, tr)]

    def arrive(ref, x, r):
        return [pull(ref, x, r, i, e[0], e[1]) for i, e in enumerate(E)]

    def tree(values):
        while len(values) > 1:
            values = [sum(values[i:i + 2]) for i in range(0, len(values), 2)]
        return values[0]

    def mix(ref, x, r, f):
        red = tree([pull(ref, x, r, key, *key) for key in RED])
        return 2.0 * red / tree(list(f)) - 1.0


    def send(ref, messages, low):
        gather_red(ref, 1 if low else lx, -1 if low else 1)
        each(messages, "x-" if low else "x+", "start")

    def take(messages, low):
        each(messages, "x+" if low else "x-", "wait_recv")

    def first_plane(x, carry):
        load_plane(x).wait()

        def step(t, carry):
            r = pl.multiple_of(t * tr, 8)
            collide(f0, x, r, [pops_ref[i, x, pl.ds(r, tr)] for i in range(19)])
            return carry

        return lax.fori_loop(0, rt, step, carry)

    lax.fori_loop(0, lx, first_plane, 0)
    each(pm0, None, "wait_recv")
    sides(False, functools.partial(colour, f0, p0), after=functools.partial(send, f0, fm0))
    loop("inner", functools.partial(colour, f0, p0))
    pack(f0, y0)
    each(fm0, "y", "start")
    each(fm0, "y", "wait_recv")
    unpack(f0, y0)

    def inner(x, r):
        f = arrive(f0, x, r)
        p1[x + 1, pl.ds(PAD + r, tr)] = mix(f0, x, r, f)
        collide(f1, x, r, f)

    loop("inner", inner)
    def edge_phase(x, r):
        p1[x + 1, pl.ds(PAD + r, tr)] = mix(f0, x, r, arrive(f0, x, r))

    sides(True, edge_phase, before=functools.partial(take, fm0),
          after=lambda low: each(pm1, "x-" if low else "x+", "start"))
    each(pm1, "y", "start")
    loop("edge", lambda x, r: collide(f1, x, r, arrive(f0, x, r)))
    each(pm1, None, "wait_recv")
    sides(False, functools.partial(colour, f1, p1), after=functools.partial(send, f1, fm1))
    loop("inner", functools.partial(colour, f1, p1))
    pack(f1, y1)
    each(fm1, "y", "start")
    each(fm1, "y", "wait_recv")
    unpack(f1, y1)

    def finish(x, r):
        f = arrive(f1, x, r)
        for i in range(19):
            out_ref[i, x, pl.ds(r, tr)] = f[i]
        phase_ref[x, pl.ds(r, tr)] = mix(f1, x, r, f)

    loop("inner", finish)
    sides(True, finish, before=functools.partial(take, fm1))
    for messages in (pm0, fm0, pm1, fm1):
        each(messages, None, "wait_send")


def solution(mesh):
    nx, ny = mesh.shape["gx"], mesh.shape["gy"]

    def on_device(populations, labels, solid_mask):
        lx, ly, lz = labels.shape
        rows = ly + 2 * PAD
        y = lax.axis_index("gy") * ly + lax.broadcasted_iota(jnp.int32, (lx, ly, lz), 1)
        solid = (solid_mask > 0) | (y == 0) | (y == ny * ly - 1)
        code = jnp.where(labels > 0, 1, 0) + jnp.where(solid, 2, 0)
        return pl.pallas_call(
            functools.partial(kernel, nx, ny),
            out_shape=(jax.ShapeDtypeStruct((19, lx, ly, lz), jnp.float32),
                       jax.ShapeDtypeStruct((lx, ly, lz), jnp.float32)),
            in_specs=[pl.BlockSpec(memory_space=pltpu.HBM), pl.BlockSpec(memory_space=pltpu.VMEM)],
            out_specs=(pl.BlockSpec(memory_space=pltpu.VMEM),) * 2,
            scratch_shapes=[
                pltpu.VMEM((lx + 2, NS, rows, lz), jnp.float32),
                pltpu.VMEM((lx + 2, NS, rows, lz), jnp.float32),
                pltpu.VMEM((lx + 2, rows, lz), jnp.float32),
                pltpu.VMEM((lx + 2, rows, lz), jnp.float32),
                pltpu.VMEM((lx, ly, lz), jnp.float32),
                pltpu.VMEM((19, lx, ly, lz), jnp.float32),
                pltpu.VMEM((4, lx, 8, lz), jnp.float32),
                pltpu.VMEM((4, lx, 8, lz), jnp.float32),
                pltpu.SemaphoreType.DMA((lx,)),
                pltpu.SemaphoreType.DMA((32,)),
                pltpu.SemaphoreType.DMA((32,)),
            ],
            compiler_params=pltpu.CompilerParams(
                collective_id=0, has_side_effects=True, vmem_limit_bytes=52 * 2**20),
        )(populations, code)

    return jax.shard_map(
        on_device, mesh=mesh,
        in_specs=(P(None, "gx", "gy", None), P("gx", "gy", None), P("gx", "gy", None)),
        out_specs=(P(None, "gx", "gy", None), P("gx", "gy", None)),
        check_vma=False)
```

```python
import functools

import jax
import jax.numpy as jnp
from jax import lax
from jax.experimental import pallas as pl
from jax.experimental.pallas import tpu as pltpu
from jax.sharding import PartitionSpec as P

E = [
    (0, 0, 0), (1, 0, 0), (-1, 0, 0), (0, 1, 0), (0, -1, 0), (0, 0, 1), (0, 0, -1),
    (1, 1, 0), (-1, -1, 0), (1, -1, 0), (-1, 1, 0), (1, 0, 1), (-1, 0, -1), (1, 0, -1),
    (-1, 0, 1), (0, 1, 1), (0, -1, -1), (0, 1, -1), (0, -1, 1),
]
OPP = [0, 2, 1, 4, 3, 6, 5, 8, 7, 10, 9, 12, 11, 14, 13, 16, 15, 18, 17]
ORDER = [
    (1, -1), 9, 1, 11, 13, (1, 0), 7, (1, 1),
    3, 15, 17, (0, 1), (-1, 1), 10,
    2, 12, 14, (-1, 0), 8, (-1, -1),
    4, 16, 18, (0, -1),
    0, 5, 6, (0, 0),
]
SLOT = {key: place for place, key in enumerate(ORDER)}
RED = [key for key in ORDER if isinstance(key, tuple)]
NS = len(ORDER)
PAD = 8
MESH = pl.DeviceIdType.MESH


def relax(f):
    def plane(pp, mm, pm, mp):
        s1, d1, s2, d2 = f[pp] + f[mm], f[pp] - f[mm], f[pm] + f[mp], f[pm] - f[mp]
        return s1 + s2, s1 - s2, d1 + d2, d1 - d2

    xy = plane(7, 8, 9, 10)
    xz = plane(11, 12, 13, 14)
    yz = plane(15, 16, 17, 18)
    sx, sy, sz = f[1] + f[2], f[3] + f[4], f[5] + f[6]
    rho = (f[0] + sx) + (sy + sz) + ((xy[0] + xz[0]) + yz[0])
    jx = (f[1] - f[2]) + (xy[2] + xz[2])
    jy = (f[3] - f[4]) + (xy[3] + yz[2])
    jz = (f[5] - f[6]) + (xz[3] + yz[3])
    inv = 1.0 / rho
    ux, uy, uz = jx * inv, jy * inv, jz * inv
    qx, qy, qz = jx * ux, jy * uy, jz * uz
    third = rho * (1.0 / 3.0)
    dxx = (sx + (xy[0] + xz[0])) - (third + qx)
    dyy = (sy + (xy[0] + yz[0])) - (third + qy)
    dzz = (sz + (xz[0] + yz[0])) - (third + qz)
    trace = (dxx + dyy) + dzz
    part = trace * (1.0 / 12.0)
    base = rho * (1.0 / 9.0) + ((qx + qy) + qz) * (1.0 / 3.0)
    tx, ty, tz = jx * (1.0 / 3.0), jy * (1.0 / 3.0), jz * (1.0 / 3.0)
    out = list(f)

    def edges(moments, rest, cross, ta, tb, pp, mm, pm, mp):
        four = (moments[0] - base) + 0.5 * rest
        a = 0.35 * four
        d = 0.3125 * (moments[1] - cross)
        b = 0.3 * (moments[2] - ta)
        c = 0.3 * (moments[3] - tb)
        p1, p2, q1, q2 = a + d, a - d, b + c, b - c
        out[pp] = f[pp] - (p1 + q1)
        out[mm] = f[mm] - (p1 - q1)
        out[pm] = f[pm] - (p2 + q2)
        out[mp] = f[mp] - (p2 - q2)
        return a, b, c

    axy, bxy, cxy = edges(xy, qz, jx * uy, tx, ty, 7, 8, 9, 10)
    axz, bxz, cxz = edges(xz, qy, jx * uz, tx, tz, 11, 12, 13, 14)
    ayz, byz, cyz = edges(yz, qx, jy * uz, ty, tz, 15, 16, 17, 18)

    def faces(delta, a, b, plus, minus):
        half = (0.625 * delta - 0.5 * part) - 2.0 * a
        diff = 2.0 * b
        out[plus] = f[plus] - (half - diff)
        out[minus] = f[minus] - (half + diff)

    faces(dxx, axy + axz, bxy + bxz, 1, 2)
    faces(dyy, axy + ayz, cxy + byz, 3, 4)
    faces(dzz, axz + ayz, cxz + cyz, 5, 6)
    out[0] = f[0] + (trace - 4.0 * ((axy + axz) + ayz))
    return out, rho


def kernel(nx, ny, pops_hbm, code_ref, out_ref, phase_ref,
           f0, f1, p0, p1, rho_ref, pops_ref, y0, y1, load_sem,
           send_sem, recv_sem):
    lx, ly, lz = code_ref.shape
    wide, narrow = [next(n for n in (size, 8) if ly % n == 0) for size in (32, 16)]
    top = PAD + ly
    gx, gy = lax.axis_index("gx"), lax.axis_index("gy")
    xp, xm = lax.rem(gx + 1, nx), lax.rem(gx + nx - 1, nx)
    up, down = gy < ny - 1, gy > 0

    barrier = pltpu.get_barrier_semaphore()

    def greet(ax, ay):
        pl.semaphore_signal(barrier, inc=1, device_id=(ax, ay), device_id_type=MESH)

    greet(xp, gy)
    greet(xm, gy)
    for flag, ay in ((up, gy + 1), (down, gy - 1)):
        @pl.when(flag)
        def _():
            greet(gx, ay)
            greet(xp, ay)
            greet(xm, ay)

    def load_plane(x):
        return pltpu.make_async_copy(pops_hbm.at[:, x], pops_ref.at[:, x], load_sem.at[x])

    for x in range(lx):
        load_plane(x).start()

    def move(ref, src, dst, k, ax, ay):
        return pltpu.make_async_remote_copy(
            src_ref=ref.at[src], dst_ref=ref.at[dst],
            send_sem=send_sem.at[k], recv_sem=recv_sem.at[k],
            device_id=(ax, ay), device_id_type=MESH)

    mid = pl.ds(PAD, ly)
    last, ghost_low = pl.ds(top - 8, 8), pl.ds(0, 8)
    first, ghost_high = pl.ds(PAD, 8), pl.ds(top, 8)
    own = pl.ds(1, lx)

    def phase_messages(ref, k):
        return [
            ("x+", move(ref, (lx, mid), (0, mid), k, xp, gy), None, None),
            ("x-", move(ref, (1, mid), (lx + 1, mid), k + 1, xm, gy), None, None),
            ("y", move(ref, (own, last), (own, ghost_low), k + 2, gx, gy + 1), up, down),
            ("y", move(ref, (own, first), (own, ghost_high), k + 3, gx, gy - 1), down, up),
            ("x+", move(ref, (lx, last), (0, ghost_low), k + 4, xp, gy + 1), up, down),
            ("x-", move(ref, (1, last), (lx + 1, ghost_low), k + 5, xm, gy + 1), up, down),
            ("x+", move(ref, (lx, first), (0, ghost_high), k + 6, xp, gy - 1), down, up),
            ("x-", move(ref, (1, first), (lx + 1, ghost_high), k + 7, xm, gy - 1), down, up),
        ]

    def field_messages(ref, rows, k):
        def s(a, b):
            return pl.ds(a, b - a)

        return [
            ("x+", move(ref, (lx, s(1, 7), mid), (0, s(1, 7), mid), k, xp, gy), None, None),
            ("x-", move(ref, (1, s(13, 19), mid), (lx + 1, s(13, 19), mid), k + 1, xm, gy),
             None, None),
            ("x+", move(ref, (lx, s(6, 8), last), (0, s(6, 8), ghost_low), k + 2, xp, gy + 1),
             up, down),
            ("x-", move(ref, (1, s(12, 14), last), (lx + 1, s(12, 14), ghost_low), k + 3, xm,
                       gy + 1), up, down),
            ("x+", move(ref, (lx, s(0, 2), first), (0, s(0, 2), ghost_high), k + 4, xp, gy - 1),
             down, up),
            ("x-", move(ref, (1, s(18, 20), first), (lx + 1, s(18, 20), ghost_high), k + 5, xm,
                       gy - 1), down, up),
            ("y", move(rows, 0, 1, k + 6, gx, gy + 1), up, down),
            ("y", move(rows, 2, 3, k + 7, gx, gy - 1), down, up),
        ]

    upward = list(range(6, 14))
    downward = list(range(18, 24)) + [0, 1]

    def pack(ref, rows):
        for flag, slots, place, row in ((up, upward, 0, top - 1), (down, downward, 2, PAD)):
            @pl.when(flag)
            def _():
                for x in range(lx):
                    for k, slot in enumerate(slots):
                        rows[place, x, k:k + 1] = ref[x + 1, slot, row:row + 1]

    def unpack(ref, rows):
        for flag, slots, place, row in ((down, upward, 1, PAD - 1), (up, downward, 3, top)):
            @pl.when(flag)
            def _():
                for x in range(lx):
                    for k, slot in enumerate(slots):
                        ref[x + 1, slot, row:row + 1] = rows[place, x, k:k + 1]

    def gather_red(ref, x, ex):
        ref[x, SLOT[(ex, 0)], PAD:top] = (
            ref[x, SLOT[(ex, 0)], PAD:top] + ref[x, SLOT[(ex, 1)], PAD - 1:top - 1]
            + ref[x, SLOT[(ex, -1)], PAD + 1:top + 1])

    def each(messages, kind, action):
        for name, copy, sends, receives in messages:
            if kind is not None and kind not in name:
                continue
            flag = receives if action == "wait_recv" else sends
            if flag is None:
                getattr(copy, action)()
            else:
                pl.when(flag)(getattr(copy, action))

    pm0, fm0 = phase_messages(p0, 0), field_messages(f0, y0, 8)
    pm1, fm1 = phase_messages(p1, 16), field_messages(f1, y1, 24)

    odd = lax.rem(gx, 2)

    def sides(near_first, body, before=None, after=None, tr=wide):
        def side(n, carry):
            pick = lax.rem(n + odd + (1 if near_first else 0), 2)
            for action in (before, body, after):
                if action is body:
                    plane = pick * (lx - 1)
                    lax.fori_loop(
                        0, ly // tr,
                        lambda t, c: body(plane, (pl.multiple_of(t * tr, 8), tr)) or c, 0)
                elif action is not None:
                    pl.when(pick == 0)(lambda: action(True))
                    pl.when(pick == 1)(lambda: action(False))
            return carry

        lax.fori_loop(0, 2, side, 0)

    def loop(kind, body, tr=wide):
        rt = ly // tr
        count = {"edge": 2, "inner": lx - 2}[kind]

        def step(t, carry):
            plane, row = t // rt, lax.rem(t, rt)
            if kind == "edge":
                plane = plane * (lx - 1)
            elif kind == "inner":
                plane = plane + 1
            body(plane, (pl.multiple_of(row * tr, 8), tr))
            return carry

        lax.fori_loop(0, count * rt, step, 0)

    zero = jnp.zeros((8, lz), jnp.float32)

    def fill(x, carry):
        for ref in (f0, f1):
            for slot in upward:
                ref[x, slot, 0:8] = zero
            for slot in downward:
                ref[x, slot, top:top + 8] = zero
        return carry

    lax.fori_loop(0, lx + 2, fill, 0)
    for ref in (f0, f1):
        for x, ex in ((0, 1), (lx + 1, -1)):
            for ey in (1, -1):
                ref[x, SLOT[(ex, ey)], PAD:top] = jnp.zeros((ly, lz), jnp.float32)
    for flag, rows in ((down, slice(0, 8)), (up, slice(top, top + 8))):
        @pl.when(jnp.logical_not(flag))
        def _():
            for ref in (p0, p1):
                for x in range(lx + 2):
                    ref[x, rows] = zero

    for x in range(lx):
        p0[1 + x, PAD:top] = jnp.where((code_ref[x] & 1) > 0, 1.0, -1.0).astype(jnp.float32)
    pl.semaphore_wait(barrier, 2 + 3 * (up.astype(jnp.int32) + down.astype(jnp.int32)))
    each(pm0, None, "start")

    def solid_at(x, r):
        return code_ref[x, pl.ds(*r)] > 1

    def collide(ref, x, r, f):
        solid = solid_at(x, r)
        relaxed, rho = relax(f)
        rho_ref[x, pl.ds(*r)] = rho
        for i in range(19):
            ref[x + 1, SLOT[i], pl.ds(PAD + r[0], r[1])] = jnp.where(solid, f[OPP[i]], relaxed[i])

    def colour(ref, pref, x, r):
        at = pl.ds(PAD + r[0], r[1])
        up_r, dn_r = pl.ds(PAD + 1 + r[0], r[1]), pl.ds(PAD - 1 + r[0], r[1])
        p = pref[x + 1, at]
        e, w = pref[x + 2, at], pref[x, at]
        n, s = pref[x + 1, up_r], pref[x + 1, dn_r]
        ne, se = pref[x + 2, up_r], pref[x + 2, dn_r]
        nw, sw = pref[x, up_r], pref[x, dn_r]

        def zsum(v):
            return pltpu.roll(v, 1, 1) + pltpu.roll(v, lz - 1, 1)

        dx, dy = e - w, n - s
        around = (e + w) + (n + s) + 2.0 * p
        ca, cb = ne - sw, se - nw
        twelfth = 1.0 / 12.0
        hx = (2.0 * dx + zsum(dx) + (ca + cb)) * twelfth
        hy = (2.0 * dy + zsum(dy) + (ca - cb)) * twelfth
        hz = (pltpu.roll(around, lz - 1, 1) - pltpu.roll(around, 1, 1)) * twelfth
        xx, yy, zz = hx * hx, hy * hy, hz * hz
        g2 = (xx + yy) + zz
        inv = lax.rsqrt(jnp.maximum(g2, 0.01))
        inv = jnp.where(solid_at(x, r), 0.0, inv)
        rho = rho_ref[x, pl.ds(*r)]
        c18 = (0.1 / 18.0) * inv
        c36 = 0.5 * c18
        k18 = (0.175 / 18.0) * (rho * (1.0 - p * p)) * inv
        k36 = 0.5 * k18
        red = 0.5 + 0.5 * p
        total, reds = {}, {}

        def read(i):
            return ref[x + 1, SLOT[i], at]

        def pair(plus, minus, square, k, along):
            shift = k * along
            for i, sign in ((plus, 1), (minus, -1)):
                value = read(i) + square
                total[i] = value
                reds[i] = red * value + shift if sign > 0 else red * value - shift

        total[0] = read(0) + (6.0 * c18) * g2
        reds[0] = red * total[0]
        pair(1, 2, c18 * (xx - g2), k18, hx)
        pair(3, 4, c18 * (yy - g2), k18, hy)
        pair(5, 6, c18 * (zz - g2), k18, hz)
        for plus, minus, along in ((7, 8, hx + hy), (9, 10, hx - hy), (11, 12, hx + hz),
                                   (13, 14, hx - hz), (15, 16, hy + hz), (17, 18, hy - hz)):
            pair(plus, minus, c36 * (along * along - g2), k36, along)
        sums = {}
        for i, (ex, ey, ez) in enumerate(E):
            value, part = total[i], reds[i]
            if ez != 0:
                value = pltpu.roll(value, ez % lz, 1)
                part = pltpu.roll(part, ez % lz, 1)
            ref[x + 1, SLOT[i], at] = value
            sums[(ex, ey)] = sums[(ex, ey)] + part if (ex, ey) in sums else part
        for key, value in sums.items():
            ref[x + 1, SLOT[key], at] = value

    def pull(ref, x, r, key, ex, ey):
        return ref[x + 1 - ex, SLOT[key], pl.ds(PAD - ey + r[0], r[1])]

    def arrive(ref, x, r):
        return [pull(ref, x, r, i, e[0], e[1]) for i, e in enumerate(E)]

    def tree(values):
        while len(values) > 1:
            values = [sum(values[i:i + 2]) for i in range(0, len(values), 2)]
        return values[0]

    def mix(ref, x, r, f):
        red = tree([pull(ref, x, r, key, *key) for key in RED])
        return 2.0 * red / tree(list(f)) - 1.0


    def send(ref, messages, low):
        gather_red(ref, 1 if low else lx, -1 if low else 1)
        each(messages, "x-" if low else "x+", "start")

    def take(messages, low):
        each(messages, "x+" if low else "x-", "wait_recv")

    def first_plane(x, carry):
        load_plane(x).wait()

        def step(t, carry):
            r = (pl.multiple_of(t * narrow, 8), narrow)
            collide(f0, x, r, [pops_ref[i, x, pl.ds(*r)] for i in range(19)])
            return carry

        return lax.fori_loop(0, ly // narrow, step, carry)

    lax.fori_loop(0, lx, first_plane, 0)
    each(pm0, None, "wait_recv")
    sides(False, functools.partial(colour, f0, p0), after=functools.partial(send, f0, fm0))
    loop("inner", functools.partial(colour, f0, p0))
    pack(f0, y0)
    each(fm0, "y", "start")
    each(fm0, "y", "wait_recv")
    unpack(f0, y0)

    def inner(x, r):
        f = arrive(f0, x, r)
        p1[x + 1, pl.ds(PAD + r[0], r[1])] = mix(f0, x, r, f)
        collide(f1, x, r, f)

    loop("inner", inner, narrow)
    def edge_phase(x, r):
        p1[x + 1, pl.ds(PAD + r[0], r[1])] = mix(f0, x, r, arrive(f0, x, r))

    sides(True, edge_phase, before=functools.partial(take, fm0),
          after=lambda low: each(pm1, "x-" if low else "x+", "start"))
    each(pm1, "y", "start")
    loop("edge", lambda x, r: collide(f1, x, r, arrive(f0, x, r)), narrow)
    each(pm1, None, "wait_recv")
    sides(False, functools.partial(colour, f1, p1), after=functools.partial(send, f1, fm1))
    loop("inner", functools.partial(colour, f1, p1))
    pack(f1, y1)
    each(fm1, "y", "start")
    each(fm1, "y", "wait_recv")
    unpack(f1, y1)

    def finish(x, r):
        f = arrive(f1, x, r)
        for i in range(19):
            out_ref[i, x, pl.ds(*r)] = f[i]
        phase_ref[x, pl.ds(*r)] = mix(f1, x, r, f)

    loop("inner", finish)
    sides(True, finish, before=functools.partial(take, fm1))
    for messages in (pm0, fm0, pm1, fm1):
        each(messages, None, "wait_send")


def solution(mesh):
    nx, ny = mesh.shape["gx"], mesh.shape["gy"]

    def on_device(populations, labels, solid_mask):
        lx, ly, lz = labels.shape
        rows = ly + 2 * PAD
        y = lax.axis_index("gy") * ly + lax.broadcasted_iota(jnp.int32, (lx, ly, lz), 1)
        solid = (solid_mask > 0) | (y == 0) | (y == ny * ly - 1)
        code = jnp.where(labels > 0, 1, 0) + jnp.where(solid, 2, 0)
        return pl.pallas_call(
            functools.partial(kernel, nx, ny),
            out_shape=(jax.ShapeDtypeStruct((19, lx, ly, lz), jnp.float32),
                       jax.ShapeDtypeStruct((lx, ly, lz), jnp.float32)),
            in_specs=[pl.BlockSpec(memory_space=pltpu.HBM), pl.BlockSpec(memory_space=pltpu.VMEM)],
            out_specs=(pl.BlockSpec(memory_space=pltpu.VMEM),) * 2,
            scratch_shapes=[
                pltpu.VMEM((lx + 2, NS, rows, lz), jnp.float32),
                pltpu.VMEM((lx + 2, NS, rows, lz), jnp.float32),
                pltpu.VMEM((lx + 2, rows, lz), jnp.float32),
                pltpu.VMEM((lx + 2, rows, lz), jnp.float32),
                pltpu.VMEM((lx, ly, lz), jnp.float32),
                pltpu.VMEM((19, lx, ly, lz), jnp.float32),
                pltpu.VMEM((4, lx, 8, lz), jnp.float32),
                pltpu.VMEM((4, lx, 8, lz), jnp.float32),
                pltpu.SemaphoreType.DMA((lx,)),
                pltpu.SemaphoreType.DMA((32,)),
                pltpu.SemaphoreType.DMA((32,)),
            ],
            compiler_params=pltpu.CompilerParams(
                collective_id=0, has_side_effects=True, vmem_limit_bytes=52 * 2**20),
        )(populations, code)

    return jax.shard_map(
        on_device, mesh=mesh,
        in_specs=(P(None, "gx", "gy", None), P("gx", "gy", None), P("gx", "gy", None)),
        out_specs=(P(None, "gx", "gy", None), P("gx", "gy", None)),
        check_vma=False)
```

```python
import functools

import jax
import jax.numpy as jnp
from jax import lax
from jax.experimental import pallas as pl
from jax.experimental.pallas import tpu as pltpu
from jax.sharding import PartitionSpec as P

E = [
    (0, 0, 0), (1, 0, 0), (-1, 0, 0), (0, 1, 0), (0, -1, 0), (0, 0, 1), (0, 0, -1),
    (1, 1, 0), (-1, -1, 0), (1, -1, 0), (-1, 1, 0), (1, 0, 1), (-1, 0, -1), (1, 0, -1),
    (-1, 0, 1), (0, 1, 1), (0, -1, -1), (0, 1, -1), (0, -1, 1),
]
OPP = [0, 2, 1, 4, 3, 6, 5, 8, 7, 10, 9, 12, 11, 14, 13, 16, 15, 18, 17]
ORDER = [
    (1, -1), 9, 1, 11, 13, (1, 0), 7, (1, 1),
    3, 15, 17, (0, 1), (-1, 1), 10,
    2, 12, 14, (-1, 0), 8, (-1, -1),
    4, 16, 18, (0, -1),
    0, 5, 6, (0, 0),
]
SLOT = {key: place for place, key in enumerate(ORDER)}
RED = [key for key in ORDER if isinstance(key, tuple)]
NS = len(ORDER)
PAD = 8
MESH = pl.DeviceIdType.MESH


def relax(f):
    def plane(pp, mm, pm, mp):
        s1, d1, s2, d2 = f[pp] + f[mm], f[pp] - f[mm], f[pm] + f[mp], f[pm] - f[mp]
        return s1 + s2, s1 - s2, d1 + d2, d1 - d2

    xy = plane(7, 8, 9, 10)
    xz = plane(11, 12, 13, 14)
    yz = plane(15, 16, 17, 18)
    sx, sy, sz = f[1] + f[2], f[3] + f[4], f[5] + f[6]
    rho = (f[0] + sx) + (sy + sz) + ((xy[0] + xz[0]) + yz[0])
    jx = (f[1] - f[2]) + (xy[2] + xz[2])
    jy = (f[3] - f[4]) + (xy[3] + yz[2])
    jz = (f[5] - f[6]) + (xz[3] + yz[3])
    inv = 1.0 / rho
    ux, uy, uz = jx * inv, jy * inv, jz * inv
    qx, qy, qz = jx * ux, jy * uy, jz * uz
    third = rho * (1.0 / 3.0)
    dxx = (sx + (xy[0] + xz[0])) - (third + qx)
    dyy = (sy + (xy[0] + yz[0])) - (third + qy)
    dzz = (sz + (xz[0] + yz[0])) - (third + qz)
    trace = (dxx + dyy) + dzz
    part = trace * (1.0 / 12.0)
    base = rho * (1.0 / 9.0) + ((qx + qy) + qz) * (1.0 / 3.0)
    tx, ty, tz = jx * (1.0 / 3.0), jy * (1.0 / 3.0), jz * (1.0 / 3.0)
    out = list(f)

    def edges(moments, rest, cross, ta, tb, pp, mm, pm, mp):
        four = (moments[0] - base) + 0.5 * rest
        a = 0.35 * four
        d = 0.3125 * (moments[1] - cross)
        b = 0.3 * (moments[2] - ta)
        c = 0.3 * (moments[3] - tb)
        p1, p2, q1, q2 = a + d, a - d, b + c, b - c
        out[pp] = f[pp] - (p1 + q1)
        out[mm] = f[mm] - (p1 - q1)
        out[pm] = f[pm] - (p2 + q2)
        out[mp] = f[mp] - (p2 - q2)
        return a, b, c

    axy, bxy, cxy = edges(xy, qz, jx * uy, tx, ty, 7, 8, 9, 10)
    axz, bxz, cxz = edges(xz, qy, jx * uz, tx, tz, 11, 12, 13, 14)
    ayz, byz, cyz = edges(yz, qx, jy * uz, ty, tz, 15, 16, 17, 18)

    def faces(delta, a, b, plus, minus):
        half = (0.625 * delta - 0.5 * part) - 2.0 * a
        diff = 2.0 * b
        out[plus] = f[plus] - (half - diff)
        out[minus] = f[minus] - (half + diff)

    faces(dxx, axy + axz, bxy + bxz, 1, 2)
    faces(dyy, axy + ayz, cxy + byz, 3, 4)
    faces(dzz, axz + ayz, cxz + cyz, 5, 6)
    out[0] = f[0] + (trace - 4.0 * ((axy + axz) + ayz))
    return out, rho


def kernel(nx, ny, pops_hbm, code_ref, out_ref, phase_ref,
           f0, f1, p0, p1, rho_ref, pops_ref, y0, y1, load_sem,
           send_sem, recv_sem):
    lx, ly, lz = code_ref.shape
    wide, narrow = [next(n for n in (size, 8) if ly % n == 0) for size in (32, 16)]
    top = PAD + ly
    gx, gy = lax.axis_index("gx"), lax.axis_index("gy")
    xp, xm = lax.rem(gx + 1, nx), lax.rem(gx + nx - 1, nx)
    up, down = gy < ny - 1, gy > 0

    barrier = pltpu.get_barrier_semaphore()

    def greet(ax, ay):
        pl.semaphore_signal(barrier, inc=1, device_id=(ax, ay), device_id_type=MESH)

    greet(xp, gy)
    greet(xm, gy)
    for flag, ay in ((up, gy + 1), (down, gy - 1)):
        @pl.when(flag)
        def _():
            greet(gx, ay)
            greet(xp, ay)
            greet(xm, ay)

    def load_plane(x):
        return pltpu.make_async_copy(pops_hbm.at[:, x], pops_ref.at[:, x], load_sem.at[x])

    for x in range(lx):
        load_plane(x).start()

    def move(ref, src, dst, k, ax, ay):
        return pltpu.make_async_remote_copy(
            src_ref=ref.at[src], dst_ref=ref.at[dst],
            send_sem=send_sem.at[k], recv_sem=recv_sem.at[k],
            device_id=(ax, ay), device_id_type=MESH)

    mid = pl.ds(PAD, ly)
    last, ghost_low = pl.ds(top - 8, 8), pl.ds(0, 8)
    first, ghost_high = pl.ds(PAD, 8), pl.ds(top, 8)
    own = pl.ds(1, lx)

    def phase_messages(ref, k):
        return [
            ("x+", move(ref, (lx, mid), (0, mid), k, xp, gy), None, None),
            ("x-", move(ref, (1, mid), (lx + 1, mid), k + 1, xm, gy), None, None),
            ("y", move(ref, (own, last), (own, ghost_low), k + 2, gx, gy + 1), up, down),
            ("y", move(ref, (own, first), (own, ghost_high), k + 3, gx, gy - 1), down, up),
            ("x+", move(ref, (lx, last), (0, ghost_low), k + 4, xp, gy + 1), up, down),
            ("x-", move(ref, (1, last), (lx + 1, ghost_low), k + 5, xm, gy + 1), up, down),
            ("x+", move(ref, (lx, first), (0, ghost_high), k + 6, xp, gy - 1), down, up),
            ("x-", move(ref, (1, first), (lx + 1, ghost_high), k + 7, xm, gy - 1), down, up),
        ]

    def field_messages(ref, rows, k):
        def s(a, b):
            return pl.ds(a, b - a)

        return [
            ("x+", move(ref, (lx, s(1, 7), mid), (0, s(1, 7), mid), k, xp, gy), None, None),
            ("x-", move(ref, (1, s(13, 19), mid), (lx + 1, s(13, 19), mid), k + 1, xm, gy),
             None, None),
            ("x+", move(ref, (lx, s(6, 8), last), (0, s(6, 8), ghost_low), k + 2, xp, gy + 1),
             up, down),
            ("x-", move(ref, (1, s(12, 14), last), (lx + 1, s(12, 14), ghost_low), k + 3, xm,
                       gy + 1), up, down),
            ("x+", move(ref, (lx, s(0, 2), first), (0, s(0, 2), ghost_high), k + 4, xp, gy - 1),
             down, up),
            ("x-", move(ref, (1, s(18, 20), first), (lx + 1, s(18, 20), ghost_high), k + 5, xm,
                       gy - 1), down, up),
            ("y", move(rows, 0, 1, k + 6, gx, gy + 1), up, down),
            ("y", move(rows, 2, 3, k + 7, gx, gy - 1), down, up),
        ]

    upward = list(range(6, 14))
    downward = list(range(18, 24)) + [0, 1]

    def pack(ref, rows):
        for flag, slots, place, row in ((up, upward, 0, top - 1), (down, downward, 2, PAD)):
            @pl.when(flag)
            def _():
                for x in range(lx):
                    for k, slot in enumerate(slots):
                        rows[place, x, k:k + 1] = ref[x + 1, slot, row:row + 1]

    def unpack(ref, rows):
        for flag, slots, place, row in ((down, upward, 1, PAD - 1), (up, downward, 3, top)):
            @pl.when(flag)
            def _():
                for x in range(lx):
                    for k, slot in enumerate(slots):
                        ref[x + 1, slot, row:row + 1] = rows[place, x, k:k + 1]

    def gather_red(ref, x, ex):
        ref[x, SLOT[(ex, 0)], PAD:top] = (
            ref[x, SLOT[(ex, 0)], PAD:top] + ref[x, SLOT[(ex, 1)], PAD - 1:top - 1]
            + ref[x, SLOT[(ex, -1)], PAD + 1:top + 1])

    def each(messages, kind, action):
        for name, copy, sends, receives in messages:
            if kind is not None and kind not in name:
                continue
            flag = receives if action == "wait_recv" else sends
            if flag is None:
                getattr(copy, action)()
            else:
                pl.when(flag)(getattr(copy, action))

    pm0, fm0 = phase_messages(p0, 0), field_messages(f0, y0, 8)
    pm1, fm1 = phase_messages(p1, 16), field_messages(f1, y1, 24)

    odd = lax.rem(gx, 2)

    def sides(near_first, body, before=None, after=None, tr=wide):
        def side(n, carry):
            pick = lax.rem(n + odd + (1 if near_first else 0), 2)
            for action in (before, body, after):
                if action is body:
                    plane = pick * (lx - 1)
                    lax.fori_loop(
                        0, ly // tr,
                        lambda t, c: body(plane, (pl.multiple_of(t * tr, 8), tr)) or c, 0)
                elif action is not None:
                    pl.when(pick == 0)(lambda: action(True))
                    pl.when(pick == 1)(lambda: action(False))
            return carry

        lax.fori_loop(0, 2, side, 0)

    def loop(kind, body, tr=wide):
        rt = ly // tr
        count = {"edge": 2, "inner": lx - 2}[kind]

        def step(t, carry):
            plane, row = t // rt, lax.rem(t, rt)
            if kind == "edge":
                plane = plane * (lx - 1)
            elif kind == "inner":
                plane = plane + 1
            body(plane, (pl.multiple_of(row * tr, 8), tr))
            return carry

        lax.fori_loop(0, count * rt, step, 0)

    def middle(body):
        if ly > 16:
            lax.fori_loop(1, lx - 1, lambda x, c: body(x, (8, ly - 16)) or c, 0)

    def border(body):
        def step(t, carry):
            body(1 + t // 2, (pl.multiple_of(lax.rem(t, 2) * (ly - 8), 8), 8))
            return carry

        lax.fori_loop(0, 2 * (lx - 2), step, 0)

    zero = jnp.zeros((8, lz), jnp.float32)

    def fill(x, carry):
        for ref in (f0, f1):
            for slot in upward:
                ref[x, slot, 0:8] = zero
            for slot in downward:
                ref[x, slot, top:top + 8] = zero
        return carry

    lax.fori_loop(0, lx + 2, fill, 0)
    for ref in (f0, f1):
        for x, ex in ((0, 1), (lx + 1, -1)):
            for ey in (1, -1):
                ref[x, SLOT[(ex, ey)], PAD:top] = jnp.zeros((ly, lz), jnp.float32)
    for flag, rows in ((down, slice(0, 8)), (up, slice(top, top + 8))):
        @pl.when(jnp.logical_not(flag))
        def _():
            for ref in (p0, p1):
                for x in range(lx + 2):
                    ref[x, rows] = zero

    for x in range(lx):
        p0[1 + x, PAD:top] = jnp.where((code_ref[x] & 1) > 0, 1.0, -1.0).astype(jnp.float32)
    pl.semaphore_wait(barrier, 2 + 3 * (up.astype(jnp.int32) + down.astype(jnp.int32)))
    each(pm0, None, "start")

    def solid_at(x, r):
        return code_ref[x, pl.ds(*r)] > 1

    def collide(ref, x, r, f):
        solid = solid_at(x, r)
        relaxed, rho = relax(f)
        rho_ref[x, pl.ds(*r)] = rho
        for i in range(19):
            ref[x + 1, SLOT[i], pl.ds(PAD + r[0], r[1])] = jnp.where(solid, f[OPP[i]], relaxed[i])

    def colour(ref, pref, x, r):
        at = pl.ds(PAD + r[0], r[1])
        up_r, dn_r = pl.ds(PAD + 1 + r[0], r[1]), pl.ds(PAD - 1 + r[0], r[1])
        p = pref[x + 1, at]
        e, w = pref[x + 2, at], pref[x, at]
        n, s = pref[x + 1, up_r], pref[x + 1, dn_r]
        ne, se = pref[x + 2, up_r], pref[x + 2, dn_r]
        nw, sw = pref[x, up_r], pref[x, dn_r]

        def zsum(v):
            return pltpu.roll(v, 1, 1) + pltpu.roll(v, lz - 1, 1)

        dx, dy = e - w, n - s
        around = (e + w) + (n + s) + 2.0 * p
        ca, cb = ne - sw, se - nw
        twelfth = 1.0 / 12.0
        hx = (2.0 * dx + zsum(dx) + (ca + cb)) * twelfth
        hy = (2.0 * dy + zsum(dy) + (ca - cb)) * twelfth
        hz = (pltpu.roll(around, lz - 1, 1) - pltpu.roll(around, 1, 1)) * twelfth
        xx, yy, zz = hx * hx, hy * hy, hz * hz
        g2 = (xx + yy) + zz
        inv = lax.rsqrt(jnp.maximum(g2, 0.01))
        inv = jnp.where(solid_at(x, r), 0.0, inv)
        rho = rho_ref[x, pl.ds(*r)]
        c18 = (0.1 / 18.0) * inv
        c36 = 0.5 * c18
        k18 = (0.175 / 18.0) * (rho * (1.0 - p * p)) * inv
        k36 = 0.5 * k18
        red = 0.5 + 0.5 * p
        total, reds = {}, {}

        def read(i):
            return ref[x + 1, SLOT[i], at]

        def pair(plus, minus, square, k, along):
            shift = k * along
            for i, sign in ((plus, 1), (minus, -1)):
                value = read(i) + square
                total[i] = value
                reds[i] = red * value + shift if sign > 0 else red * value - shift

        total[0] = read(0) + (6.0 * c18) * g2
        reds[0] = red * total[0]
        pair(1, 2, c18 * (xx - g2), k18, hx)
        pair(3, 4, c18 * (yy - g2), k18, hy)
        pair(5, 6, c18 * (zz - g2), k18, hz)
        for plus, minus, along in ((7, 8, hx + hy), (9, 10, hx - hy), (11, 12, hx + hz),
                                   (13, 14, hx - hz), (15, 16, hy + hz), (17, 18, hy - hz)):
            pair(plus, minus, c36 * (along * along - g2), k36, along)
        sums = {}
        for i, (ex, ey, ez) in enumerate(E):
            value, part = total[i], reds[i]
            if ez != 0:
                value = pltpu.roll(value, ez % lz, 1)
                part = pltpu.roll(part, ez % lz, 1)
            ref[x + 1, SLOT[i], at] = value
            sums[(ex, ey)] = sums[(ex, ey)] + part if (ex, ey) in sums else part
        for key, value in sums.items():
            ref[x + 1, SLOT[key], at] = value

    def pull(ref, x, r, key, ex, ey):
        return ref[x + 1 - ex, SLOT[key], pl.ds(PAD - ey + r[0], r[1])]

    def arrive(ref, x, r):
        return [pull(ref, x, r, i, e[0], e[1]) for i, e in enumerate(E)]

    def tree(values):
        while len(values) > 1:
            values = [sum(values[i:i + 2]) for i in range(0, len(values), 2)]
        return values[0]

    def mix(ref, x, r, f):
        red = tree([pull(ref, x, r, key, *key) for key in RED])
        return 2.0 * red / tree(list(f)) - 1.0


    def send(ref, messages, low):
        gather_red(ref, 1 if low else lx, -1 if low else 1)
        each(messages, "x-" if low else "x+", "start")

    def take(messages, low):
        each(messages, "x+" if low else "x-", "wait_recv")

    def first_plane(x, carry):
        load_plane(x).wait()

        def step(t, carry):
            r = (pl.multiple_of(t * narrow, 8), narrow)
            collide(f0, x, r, [pops_ref[i, x, pl.ds(*r)] for i in range(19)])
            return carry

        return lax.fori_loop(0, ly // narrow, step, carry)

    lax.fori_loop(0, lx, first_plane, 0)
    each(pm0, None, "wait_recv")
    sides(False, functools.partial(colour, f0, p0), after=functools.partial(send, f0, fm0))
    loop("inner", functools.partial(colour, f0, p0))
    pack(f0, y0)
    each(fm0, "y", "start")

    def inner(x, r):
        f = arrive(f0, x, r)
        p1[x + 1, pl.ds(PAD + r[0], r[1])] = mix(f0, x, r, f)
        collide(f1, x, r, f)

    middle(inner)
    each(fm0, "y", "wait_recv")
    unpack(f0, y0)
    border(inner)

    def edge_phase(x, r):
        p1[x + 1, pl.ds(PAD + r[0], r[1])] = mix(f0, x, r, arrive(f0, x, r))

    sides(True, edge_phase, before=functools.partial(take, fm0),
          after=lambda low: each(pm1, "x-" if low else "x+", "start"))
    each(pm1, "y", "start")
    loop("edge", lambda x, r: collide(f1, x, r, arrive(f0, x, r)), narrow)
    each(pm1, None, "wait_recv")
    sides(False, functools.partial(colour, f1, p1), after=functools.partial(send, f1, fm1))
    loop("inner", functools.partial(colour, f1, p1))
    pack(f1, y1)
    each(fm1, "y", "start")

    def finish(x, r):
        f = arrive(f1, x, r)
        for i in range(19):
            out_ref[i, x, pl.ds(*r)] = f[i]
        phase_ref[x, pl.ds(*r)] = mix(f1, x, r, f)

    middle(finish)
    each(fm1, "y", "wait_recv")
    unpack(f1, y1)
    border(finish)

    sides(True, finish, before=functools.partial(take, fm1))
    for messages in (pm0, fm0, pm1, fm1):
        each(messages, None, "wait_send")


def solution(mesh):
    nx, ny = mesh.shape["gx"], mesh.shape["gy"]

    def on_device(populations, labels, solid_mask):
        lx, ly, lz = labels.shape
        rows = ly + 2 * PAD
        y = lax.axis_index("gy") * ly + lax.broadcasted_iota(jnp.int32, (lx, ly, lz), 1)
        solid = (solid_mask > 0) | (y == 0) | (y == ny * ly - 1)
        code = jnp.where(labels > 0, 1, 0) + jnp.where(solid, 2, 0)
        return pl.pallas_call(
            functools.partial(kernel, nx, ny),
            out_shape=(jax.ShapeDtypeStruct((19, lx, ly, lz), jnp.float32),
                       jax.ShapeDtypeStruct((lx, ly, lz), jnp.float32)),
            in_specs=[pl.BlockSpec(memory_space=pltpu.HBM), pl.BlockSpec(memory_space=pltpu.VMEM)],
            out_specs=(pl.BlockSpec(memory_space=pltpu.VMEM),) * 2,
            scratch_shapes=[
                pltpu.VMEM((lx + 2, NS, rows, lz), jnp.float32),
                pltpu.VMEM((lx + 2, NS, rows, lz), jnp.float32),
                pltpu.VMEM((lx + 2, rows, lz), jnp.float32),
                pltpu.VMEM((lx + 2, rows, lz), jnp.float32),
                pltpu.VMEM((lx, ly, lz), jnp.float32),
                pltpu.VMEM((19, lx, ly, lz), jnp.float32),
                pltpu.VMEM((4, lx, 8, lz), jnp.float32),
                pltpu.VMEM((4, lx, 8, lz), jnp.float32),
                pltpu.SemaphoreType.DMA((lx,)),
                pltpu.SemaphoreType.DMA((32,)),
                pltpu.SemaphoreType.DMA((32,)),
            ],
            compiler_params=pltpu.CompilerParams(
                collective_id=0, has_side_effects=True, vmem_limit_bytes=52 * 2**20),
        )(populations, code)

    return jax.shard_map(
        on_device, mesh=mesh,
        in_specs=(P(None, "gx", "gy", None), P("gx", "gy", None), P("gx", "gy", None)),
        out_specs=(P(None, "gx", "gy", None), P("gx", "gy", None)),
        check_vma=False)
```
